256 devices in a mesh: tm: 32 (over x, z_lo, core), height: 8 (over y, z_hi).
Axes of the slice: x: 4, y: 4, z: 8 (z_hi: 2, z_lo: 4; z = z_hi * 4 + z_lo), core: 2. Of those that a mesh axis runs over, the one named last changes fastest.
Arguments:
- feats: bfloat16 [96, 16, 96, 192], P('tm', 'height'), may hold values from -6 to 6
- conv_weight: bfloat16 [3, 3, 3, 192, 192], replicated, may hold values from -0.078125 to 0.078125
- conv_bias: float32 [192], replicated, may hold values from -3 to 3
- patch_weight: bfloat16 [768, 1536], replicated, may hold values from -0.21875 to 0.21875
- patch_bias: float32 [1536], replicated, may hold values from -3 to 3
- time_weight: float32 [256, 4608], replicated, may hold values from -0.375 to 0.375
- qkv_weight: bfloat16 [3, 1536, 1024], P(None, None, 'height')
- out_weight: bfloat16 [1024, 1536], P('height'), may hold values from -0.1875 to 0.1875
- steps_index: int32 [32], P('tm'), may hold values from 0 to 999
- lookback: int32 [32], P('tm'), may hold values from 0 to 8, as said below
Outputs:
- refined: bfloat16 [96, 8, 48, 1536], P('tm', 'height')
The draws below stay inside these ranges and needn't reach their ends.
Inputs may be any that keep to these rules, and one draw needn't show every extreme that they name: lookback of group k is at most k; the last group looks back 8 groups.
All inputs are finite; a program needn't handle non-finite values.
Results may differ from the reference program's by a relative error of at most 0.018.
Values may be sent and summed in bfloat16 or wider, within the bound.
A program may use at most 128 MiB of HBM per device.

```python
import math
import jax
import jax.numpy as jnp
from jax import lax

D = 1536
HEADS = 8
HD = 128
CC = 192
FREQ = 256
FR = 3
WIN = 8
GROUPS = 32
FRAMES = 96
LROWS = 16
LCOLS = 96


def draw_qkv_weight(key, part):
    key = jax.random.fold_in(key, 11)
    first = jax.random.fold_in(key, 0)
    columns = HEADS * HD
    drawn = jax.random.normal(first, (3, D, columns), jnp.float32) * D ** (-0.5)
    return drawn.astype(jnp.bfloat16)


def draw_lookback(key, part):
    key = jax.random.fold_in(key, 23)
    raw = jax.random.randint(key, (GROUPS,), 0, WIN + 1, jnp.int32)
    positions = jnp.arange(GROUPS).astype(jnp.int32)
    bounded = jnp.minimum(raw, positions)
    return jnp.where(positions == GROUPS - 1, WIN, bounded).astype(jnp.int32)


def set_ends(values, rng, low, largest):
    longest = values.shape.index(max(values.shape))
    spots = []
    for shift in (0, 1):
        where = [jax.random.randint(jax.random.fold_in(rng, axis), (), 0, length) for axis, length in enumerate(values.shape)]
        where[longest] = (where[longest] + shift) % values.shape[longest]
        spots.append(tuple(where))
    return values.at[spots[0]].set(low).at[spots[1]].set(largest)


def level_of(rng, extent, shards, smallest, largest):
    def one(dim, parts):
        steps = jax.random.uniform(jax.random.fold_in(jax.random.fold_in(rng, 6), dim), (parts,), jnp.float32, smallest / len(shards), largest / len(shards))
        return jnp.repeat(jnp.exp(steps), extent[dim] // parts).reshape((-1,) + (1,) * (len(extent) - dim - 1))

    factor_of = one(*shards[0])
    for cut in shards[1:]:
        factor_of = factor_of * one(*cut)
    return factor_of


def gaussian(own_key, shape, width, reach, shards=(), dtype=jnp.bfloat16):
    values = width * jax.random.normal(own_key, shape, jnp.float32)
    if shards:
        values = values * level_of(own_key, shape, shards, -0.22, 0.18)
    return jnp.clip(values, -reach, reach).astype(dtype)


def setup_inputs(seed: int = 0) -> dict:
    seeds = jax.random.split(jax.random.key(seed), 11)
    return {
        "feats": gaussian(seeds[0], (FRAMES, LROWS, LCOLS, CC), 1.0, 6.0, ((0, 32), (1, 8))),
        "conv_weight": gaussian(seeds[1], (3, 3, 3, CC, CC), (27 * CC) ** -0.5, 0.078125),
        "conv_bias": gaussian(seeds[2], (CC,), 0.5, 3.0, (), jnp.float32),
        "patch_weight": gaussian(seeds[3], (4 * CC, D), (4 * CC) ** -0.5, 0.21875),
        "patch_bias": gaussian(seeds[4], (D,), 0.5, 3.0, (), jnp.float32),
        "time_weight": gaussian(seeds[5], (FREQ, 3 * D), FREQ ** -0.5, 0.375, (), jnp.float32),
        "qkv_weight": draw_qkv_weight(jax.random.fold_in(seeds[10], 71), 0),
        "out_weight": gaussian(seeds[7], (HEADS * HD, D), (HEADS * HD) ** -0.5, 0.1875, ((0, 8),)),
        "steps_index": set_ends(jax.random.randint(seeds[8], (GROUPS,), 0, 1000), jax.random.fold_in(seeds[8], 1), 0, 999).astype(jnp.int32),
        "lookback": draw_lookback(jax.random.fold_in(seeds[10], 71), 0),
    }


def causal_conv(padded, conv_weight, frames, lat_rows, lat_cols):
    channels = padded.shape[-1]
    summed = jnp.zeros((frames * lat_rows * lat_cols, conv_weight.shape[-1]), jnp.float32)
    for tshift in range(3):
        time_slab = padded[tshift:tshift + frames]
        tap_stack = jnp.concatenate([time_slab[:, rshift:rshift + lat_rows, cshift:cshift + lat_cols, :] for rshift in range(3) for cshift in range(3)], axis=-1)
        summed = summed + jnp.dot(tap_stack.reshape(-1, 9 * channels), conv_weight[tshift].reshape(9 * channels, -1), preferred_element_type=jnp.float32)
    return summed

def embed_time(steps_value, freq_dim):
    half_dim = freq_dim // 2
    frequencies = jnp.exp(-math.log(10000.0) * jnp.arange(half_dim).astype(jnp.float32) / half_dim)
    angles = steps_value.astype(jnp.float32)[:, None] * frequencies[None, :]
    return jnp.concatenate([jnp.cos(angles), jnp.sin(angles)], axis=1)

def reference(feats, conv_weight, conv_bias, patch_weight, patch_bias, time_weight, qkv_weight, out_weight, steps_index, lookback):
    frames, lat_rows, lat_cols, channels = feats.shape
    padded = jnp.pad(feats, ((2, 0), (1, 1), (1, 1), (0, 0)))
    conv_out = causal_conv(padded, conv_weight, frames, lat_rows, lat_cols) + conv_bias
    activated = jax.nn.silu(conv_out).astype(jnp.bfloat16)
    tok_rows = lat_rows // 2
    tok_cols = lat_cols // 2
    patches = activated.reshape(frames, tok_rows, 2, tok_cols, 2, channels).transpose(0, 1, 3, 2, 4, 5).reshape(-1, 4 * channels)
    tokens = (jnp.dot(patches, patch_weight, preferred_element_type=jnp.float32) + patch_bias).astype(jnp.bfloat16)
    model_width = patch_weight.shape[1]
    ntok = FR * tok_rows * tok_cols
    embedding = embed_time(steps_index, time_weight.shape[0])
    modulation = jnp.dot(embedding, time_weight, precision=lax.Precision.HIGHEST)
    shift_rows = modulation[:, None, :model_width]
    scale_rows = modulation[:, None, model_width:2 * model_width]
    gate_rows = modulation[:, None, 2 * model_width:]
    widened = lax.optimization_barrier(tokens).astype(jnp.float32).reshape(GROUPS, ntok, model_width)
    row_mean = lax.optimization_barrier(jnp.mean(widened, axis=-1, keepdims=True))
    centered = widened - row_mean
    variance = lax.optimization_barrier(jnp.mean(centered * centered, axis=-1, keepdims=True))
    normed = (centered * lax.rsqrt(variance + 1e-06) * (1.0 + scale_rows) + shift_rows).astype(jnp.bfloat16)
    projected = jnp.einsum('ctd,sdh->scth', normed.astype(jnp.float32), qkv_weight.astype(jnp.float32)).astype(jnp.bfloat16)
    projected = lax.optimization_barrier(projected).astype(jnp.float32).reshape(3, GROUPS, ntok, HEADS, HD)
    queries = projected[0]
    key_pad = jnp.pad(projected[1], ((WIN, 0), (0, 0), (0, 0), (0, 0)))
    value_pad = jnp.pad(projected[2], ((WIN, 0), (0, 0), (0, 0), (0, 0)))
    score_scale = HD ** (-0.5)

    def one_group(group_index):
        group_queries = queries[group_index]
        key_block = lax.dynamic_slice_in_dim(key_pad, group_index, WIN + 1, 0).reshape(-1, HEADS, HD)
        value_block = lax.dynamic_slice_in_dim(value_pad, group_index, WIN + 1, 0).reshape(-1, HEADS, HD)
        offsets = WIN - jnp.arange(WIN + 1).astype(jnp.int32)
        allowed = jnp.repeat(offsets <= lookback[group_index], ntok)
        scores = jnp.einsum('qhd,khd->hqk', group_queries, key_block) * score_scale
        scores = jnp.where(allowed, scores, -1e+30)
        top = lax.optimization_barrier(jnp.max(scores, axis=-1, keepdims=True))
        probs = jnp.where(allowed, jnp.exp(scores - top), 0.0)
        totals = lax.optimization_barrier(jnp.sum(probs, axis=-1))
        weights = lax.optimization_barrier(probs.astype(jnp.bfloat16)).astype(jnp.float32)
        mixed = jnp.einsum('hqk,khd->qhd', weights, value_block) / totals.T[:, :, None]
        return mixed.astype(jnp.bfloat16).reshape(ntok, HEADS * HD)
    heads_out = lax.map(one_group, jnp.arange(GROUPS).astype(jnp.int32))
    attended = jnp.dot(heads_out.reshape(-1, HEADS * HD), out_weight, preferred_element_type=jnp.float32).reshape(GROUPS, ntok, model_width)
    refined = (widened + gate_rows * attended).astype(jnp.bfloat16)
    return refined.reshape(frames, tok_rows, tok_cols, model_width)
```

```python
import math

import jax
import jax.numpy as jnp
import numpy as np
from jax import lax
from jax.experimental import pallas as pl
from jax.experimental.pallas import tpu as pltpu
from jax.sharding import PartitionSpec as P

HD = 128
WIN = 8
D = 1536
CC = 192
FREQ = 256
ROW = 144
HALF = 4 * ROW
NTOK = 8 * ROW
QB = 288
NEG = -1e30
MESH = pl.DeviceIdType.MESH
F32 = jnp.float32
BF16 = jnp.bfloat16


def kernel(
    feats, conv_w, conv_b, patch_w, patch_b, time_w, qkv_w, out_w, steps, lookback, phi,
    out,
    fp, cw, pw, tw, wq, ow, phv, conv_acc, act, pat, tok, mod, q_ref, kv, acc, row_max, row_sum, obuf, mix,
    load_sem, fetch_sem, halo_send, halo_recv, pat_send, pat_recv, win_send, win_recv, fwd_send, mate_send,
    ow_send, ow_recv, mix_send, mix_recv,
):
    tm = lax.axis_index("tm")
    h = lax.axis_index("height")
    x = tm // 8
    zl = (tm // 2) % 4
    c = tm % 2
    y = h // 2
    zh = h % 2

    def dev(x_, zl_, c_, y_, zh_):
        return (x_ * 8 + zl_ * 2 + c_, y_ * 2 + zh_)

    def remote(src, dst, send, recv, to):
        return pltpu.make_async_remote_copy(
            src_ref=src, dst_ref=dst, send_sem=send, recv_sem=recv, device_id=to, device_id_type=MESH
        )

    loads = [
        pltpu.make_async_copy(conv_w, cw, load_sem.at[0]),
        pltpu.make_async_copy(feats, fp.at[pl.ds(2, 3), pl.ds(1, 2)], load_sem.at[1]),
        pltpu.make_async_copy(patch_w, pw, load_sem.at[2]),
        pltpu.make_async_copy(time_w, tw, load_sem.at[3]),
        pltpu.make_async_copy(phi, phv, load_sem.at[4]),
    ]
    for part in range(3):
        loads.append(
            pltpu.make_async_copy(qkv_w.at[part], wq.at[:, pl.ds(part * HD, HD)], load_sem.at[5 + part])
        )
    loads.append(pltpu.make_async_copy(out_w, ow.at[h], load_sem.at[8]))
    for cp in loads:
        cp.start()

    tm_next, tm_prev = (tm + 1) % 32, (tm + 31) % 32
    h_next, h_prev = (h + 1) % 8, (h + 7) % 8
    partners = [(tm, (h + k) % 8) for k in range(1, 8)]
    partners += [(t, r) for t in (tm_next, tm_prev) for r in (h_prev, h, h_next)]
    partners += [dev(x, (zl + k) % 4, c, y, zh) for k in (1, 3)]
    partners += [dev((x + k) % 4, zl, c, y, zh) for k in (1, 3)]
    partners += [dev(x, zl, 1 - c, y, zh)]
    partners += [dev(x, (zl + k) % 4, c, y, 1 - zh) for k in (1, 2, 3)]
    barrier = pltpu.get_barrier_semaphore()
    for to in partners:
        pl.semaphore_signal(barrier, inc=1, device_id=to, device_id_type=MESH)
    pl.semaphore_wait(barrier, len(partners))

    halo = [
        (feats.at[:, pl.ds(1, 1)], fp.at[pl.ds(2, 3), pl.ds(0, 1)], (tm, h_next)),
        (feats.at[:, pl.ds(0, 1)], fp.at[pl.ds(2, 3), pl.ds(3, 1)], (tm, h_prev)),
        (feats.at[pl.ds(1, 2)], fp.at[pl.ds(0, 2), pl.ds(1, 2)], (tm_next, h)),
        (feats.at[pl.ds(1, 2), pl.ds(1, 1)], fp.at[pl.ds(0, 2), pl.ds(0, 1)], (tm_next, h_next)),
        (feats.at[pl.ds(1, 2), pl.ds(0, 1)], fp.at[pl.ds(0, 2), pl.ds(3, 1)], (tm_next, h_prev)),
    ]
    halo = [remote(s, d, halo_send.at[i], halo_recv.at[i], to) for i, (s, d, to) in enumerate(halo)]
    for cp in halo:
        cp.start()

    loads[4].wait()
    loads[3].wait()
    angle = steps[0].astype(F32) * phv[...]
    embedding = jnp.concatenate([jnp.cos(angle), jnp.sin(angle)], axis=0)
    for part in range(3):
        for tile in range(D // 128):
            lane = part * D + tile * 128
            mod[part : part + 1, tile * 128 : (tile + 1) * 128] = jnp.sum(
                tw[:, lane : lane + 128] * embedding, axis=0, keepdims=True
            )

    conv_acc[...] = jnp.zeros_like(conv_acc)
    loads[0].wait()
    loads[1].wait()
    for cp in halo:
        cp.wait_recv()

    @pl.when(h == 0)
    def _():
        fp[:, 0:1] = jnp.zeros((5, 1, 96, CC), BF16)

    @pl.when(h == 7)
    def _():
        fp[:, 3:4] = jnp.zeros((5, 1, 96, CC), BF16)

    @pl.when(tm == 0)
    def _():
        fp[0:2] = jnp.zeros((2, 4, 96, CC), BF16)

    def conv_tap(ab, _):
        rows = fp[pl.ds(ab // 3, 3), pl.ds(ab % 3, 2)].reshape(6 * 96, CC)
        for e in range(3):
            term = jnp.dot(rows, cw[ab // 3, ab % 3, e], preferred_element_type=F32)
            conv_acc[e, :, 8:104] += term.reshape(6, 96, CC)
        return 0

    lax.fori_loop(0, 9, conv_tap, 0)
    own = zh * 4 + y
    for s in range(6):
        v = conv_acc[0, s, 7:103] + conv_acc[1, s, 8:104] + conv_acc[2, s, 9:105] + conv_b[...]
        v = v / (1.0 + jnp.exp(-v))
        act[0, s] = v[:, 0:128]
        act[1, s, :, 0:64] = v[:, 128:192]
    for f in range(3):
        pieces = []
        for u in range(2):
            for w in range(2):
                columns = pl.ds(w, 48, stride=2)
                pieces += [act[0, 2 * f + u, columns, :], act[1, 2 * f + u, columns, :][:, :64]]
        pat[own, pl.ds(48 * f, 48)] = jnp.concatenate(pieces, axis=1).astype(BF16)

    def y_sends(slot, first):
        return [
            remote(pat.at[slot], pat.at[slot], pat_send.at[first + k], pat_recv.at[slot], (tm, ((y + k + 1) % 4) * 2 + zh))
            for k in (0, 2, 1)
        ]

    other = (1 - zh) * 4 + y
    z_send = remote(pat.at[own], pat.at[own], pat_send.at[6], pat_recv.at[own], (tm, y * 2 + 1 - zh))
    z_send.start()
    own_sends = y_sends(own, 0)
    for cp in own_sends:
        cp.start()
    for cp in loads[5:8]:
        cp.wait()
    loads[2].wait()

    def pat_wait(slot):
        pltpu.make_async_remote_copy(
            src_ref=pat.at[slot], dst_ref=pat.at[slot], send_sem=pat_send.at[0], recv_sem=pat_recv.at[slot],
            device_id=(tm, h_next), device_id_type=MESH,
        ).wait_recv()

    shift_row = mod[0:1, :]
    scale_row = 1.0 + mod[1:2, :]
    q_scale = HD ** (-0.5) * math.log2(math.e)

    def project(slot):
        tokens = (jnp.dot(pat[slot], pw[...], preferred_element_type=F32) + patch_b[...]).astype(BF16)

        @pl.when(slot == own)
        def _():
            tok[...] = tokens

        wide = tokens.astype(F32)
        centered = wide - jnp.mean(wide, axis=-1, keepdims=True)
        variance = jnp.mean(centered * centered, axis=-1, keepdims=True)
        normed = (centered * lax.rsqrt(variance + 1e-06) * scale_row + shift_row).astype(BF16)
        qkv = jnp.dot(normed, wq[...], preferred_element_type=F32)
        rows = pl.ds(pl.multiple_of(slot * ROW, ROW), ROW)
        q_ref[rows, :] = (qkv[:, 0:HD] * q_scale).astype(BF16)
        kv[0, 0, rows, :] = qkv[:, HD : 2 * HD].astype(BF16)
        kv[0, 1, rows, :] = qkv[:, 2 * HD :].astype(BF16)

    def half_rows(g):
        return pl.ds(pl.multiple_of(((zh + g) % 2) * HALF, HALF), HALF)

    def half_of(slot, g):
        return kv.at[slot, :, half_rows(g), :]

    z_next = dev(x, (zl + 1) % 4, c, y, zh)
    z_prev = dev(x, (zl + 3) % 4, c, y, zh)
    x_next = dev((x + 1) % 4, zl, c, y, zh)
    mate = dev(x, zl, 1 - c, y, zh)

    win_copies = []
    for g in range(2):
        if g == 0:
            project(own)
        else:
            pat_wait(other)
            other_sends = y_sends(other, 3)
            for cp in other_sends:
                cp.start()
            project(other)

        def step(k, _, g=g):
            slot = ((zh + g) % 2) * 4 + (y + k + k // 2 - 2 * (k // 3)) % 4
            pat_wait(slot)
            project(slot)
            return 0

        lax.fori_loop(1, 4, step, 0)
        up = remote(half_of(0, g), half_of(1, g), win_send.at[g], win_recv.at[1, g], z_next)
        across = remote(half_of(0, g), half_of(4, g), win_send.at[2 + g], win_recv.at[4, g], x_next)
        across.start()

        @pl.when(zl < 3)
        def _(up=up):
            up.start()

        win_copies.append((up, across))

    loads[8].wait()
    ow_near = dev(x, 3 * (1 - zl // 3), c, y, 1 - zh)
    ow_far = dev(x, 1 + (1 - zl // 3), c, y, 1 - zh)
    ow_z = [
        remote(ow.at[h], ow.at[h], ow_send.at[6 + i], ow_recv.at[h], to) for i, to in enumerate((ow_near, ow_far))
    ]

    @pl.when((zl % 3) == 0)
    def _():
        for cp in ow_z:
            cp.start()

    def ow_sends(row, first):
        return [
            remote(ow.at[row], ow.at[row], ow_send.at[first + k], ow_recv.at[row], (tm, ((y + k + 1) % 4) * 2 + zh))
            for k in (0, 2, 1)
        ]

    ow_own = ow_sends(h, 0)
    for cp in ow_own:
        cp.start()
    h_other = y * 2 + 1 - zh

    def ow_wait(row):
        pltpu.make_async_remote_copy(
            src_ref=ow.at[row], dst_ref=ow.at[row], send_sem=ow_send.at[0], recv_sem=ow_recv.at[row],
            device_id=(tm, h_next), device_id_type=MESH,
        ).wait_recv()

    acc[...] = jnp.zeros_like(acc)
    row_sum[...] = jnp.zeros_like(row_sum)
    row_max[...] = jnp.full_like(row_max, NEG)

    def attend(slot, g, back):
        penalty = jnp.where(back <= lookback[0], 0.0, 1e30)
        keys = kv[slot, 0, half_rows(g), :]
        values = kv[slot, 1, half_rows(g), :]

        def block(i, _):
            rows = pl.ds(pl.multiple_of(i * QB, QB), QB)
            scores = lax.dot_general(
                q_ref[rows, :], keys, (((1,), (1,)), ((), ())), preferred_element_type=F32
            )
            old = row_max[rows, :]
            new = jnp.maximum(old, jnp.max(scores, axis=1, keepdims=True) - penalty)
            probs = jnp.exp2(scores - (new[:, 0:1] + penalty))
            shrink = jnp.exp2(old - new)
            row_max[rows, :] = new
            row_sum[rows, :] = row_sum[rows, :] * shrink + jnp.sum(probs, axis=1, keepdims=True)
            acc[rows, :] = acc[rows, :] * shrink + jnp.dot(
                probs.astype(BF16), values, preferred_element_type=F32
            )
            return 0

        lax.fori_loop(0, NTOK // QB, block, 0)

    def own_half(g, _):
        attend(0, g, 0)
        return 0

    lax.fori_loop(0, 2, own_half, 0)

    def coded(order):
        return sum(((d - 1) * 2 + g) * 8**i for i, (d, g) in enumerate(order))

    a, b = 0, 1
    orders = [
        [(4, a), (4, b), (3, a), (3, b), (2, a), (2, b), (1, a), (1, b)],
        [(1, a), (4, a), (1, b), (4, b), (3, a), (3, b), (2, a), (2, b)],
        [(1, a), (4, a), (1, b), (4, b), (3, a), (2, a), (3, b), (2, b)],
        [(1, a), (4, a), (1, b), (4, b), (2, a), (2, b), (3, a), (3, b)],
    ]
    is0, is3 = (3 - zl) // 3, zl // 3
    is2 = zl // 2 - is3
    is1 = 1 - is0 - is2 - is3
    code = sum(i * coded(o) for i, o in zip((is0, is1, is2, is3), orders))

    def event_copies(i, code):
        digit = code % 8
        d, g = digit // 2 + 1, digit % 2
        up = remote(half_of(d, g), half_of((d + 1) % 5, g), fwd_send.at[i], win_recv.at[(d + 1) % 5, g], z_next)
        down = remote(half_of(d, g), half_of(d - 1, g), fwd_send.at[i], win_recv.at[d - 1, g], z_prev)
        src = c * d + (1 - c) * (d % 4)
        dst = 4 + c * d + (1 - c) * (d % 4 + 1)
        got = 4 + (1 - c) * d + c * (d % 4 + 1)
        share = remote(half_of(src, g), half_of(dst, g), mate_send.at[i], win_recv.at[dst, g], mate)
        goes_up = jnp.logical_and(d <= zl, zl < 3)
        goes_down = jnp.logical_and(d > zl, zl > 0)
        return d, g, up, down, share, got, goes_up, goes_down

    def event(i, code):
        d, g, up, down, share, got, goes_up, goes_down = event_copies(i, code)
        remote(half_of(0, g), half_of(d, g), fwd_send.at[i], win_recv.at[d, g], mate).wait_recv()

        @pl.when(goes_up)
        def _():
            up.start()

        @pl.when(goes_down)
        def _():
            down.start()

        share.start()
        attend(d, g, 2 * d)
        remote(half_of(0, g), half_of(got, g), mate_send.at[i], win_recv.at[got, g], mate).wait_recv()
        attend(got, g, 2 * (got - 4) - 1)
        return code // 8

    code_mid = lax.fori_loop(0, 3, event, code)
    ow_wait(h_other)
    ow_more = ow_sends(h_other, 3)
    for cp in ow_more:
        cp.start()
    lax.fori_loop(3, 8, event, code_mid)

    def finish(s, _):
        rows = pl.ds(pl.multiple_of(s * ROW, ROW), ROW)
        heads_out = (acc[rows, :] / row_sum[rows, :]).astype(BF16)
        obuf[s] = heads_out
        to = (s % 4) * 2 + s // 4

        @pl.when(to == h)
        def _():
            mix[h] = heads_out

        @pl.when(to != h)
        def _():
            remote(obuf.at[s], mix.at[h], mix_send.at[s], mix_recv.at[h], (tm, to)).start()

        return 0

    lax.fori_loop(0, 8, finish, 0)
    for k in range(1, 4):
        for half in range(2):
            ow_wait(((y + k) % 4) * 2 + half)
    for k in range(1, 8):
        r = (h + k) % 8
        remote(obuf.at[0], mix.at[r], mix_send.at[0], mix_recv.at[r], (tm, h_next)).wait_recv()
    heads = jnp.concatenate([mix[i] for i in range(8)], axis=1)
    attended = jnp.dot(heads, ow[...].reshape(8 * HD, D), preferred_element_type=F32)
    refined = (tok[...].astype(F32) + mod[2:3, :] * attended).astype(BF16)
    out[...] = refined.reshape(3, 1, 48, D)

    for cp in halo + own_sends + other_sends + [z_send] + ow_own + ow_more:
        cp.wait_send()

    @pl.when((zl % 3) == 0)
    def _():
        for cp in ow_z:
            cp.wait_send()

    for up, across in win_copies:
        across.wait_send()

        @pl.when(zl < 3)
        def _(up=up):
            up.wait_send()

    def drain(i, code):
        _, _, up, down, share, _, goes_up, goes_down = event_copies(i, code)

        @pl.when(goes_up)
        def _():
            up.wait_send()

        @pl.when(goes_down)
        def _():
            down.wait_send()

        share.wait_send()
        return code // 8

    lax.fori_loop(0, 8, drain, code)

    def drain_mix(s, _):
        to = (s % 4) * 2 + s // 4

        @pl.when(to != h)
        def _():
            remote(obuf.at[s], mix.at[h], mix_send.at[s], mix_recv.at[h], (tm, to)).wait_send()

        return 0

    lax.fori_loop(0, 8, drain_mix, 0)


def on_device(
    feats, conv_weight, conv_bias, patch_weight, patch_bias, time_weight, qkv_weight, out_weight, steps_index, lookback
):
    half = FREQ // 2
    freq = np.exp(np.float32(-math.log(10000.0)) * np.arange(half, dtype=np.float32) / np.float32(half))
    phi = jnp.asarray(np.broadcast_to(freq.astype(np.float32)[:, None], (half, 128)))
    vmem = pl.BlockSpec(memory_space=pltpu.VMEM)
    smem = pl.BlockSpec(memory_space=pltpu.SMEM)
    hbm = pl.BlockSpec(memory_space=pl.ANY)
    dma = pltpu.SemaphoreType.DMA
    return pl.pallas_call(
        kernel,
        out_shape=jax.ShapeDtypeStruct((3, 1, 48, D), BF16),
        in_specs=[hbm, hbm, vmem, hbm, vmem, hbm, hbm, hbm, smem, smem, hbm],
        out_specs=vmem,
        scratch_shapes=[
            pltpu.VMEM((5, 4, 96, CC), BF16),
            pltpu.VMEM((3, 3, 3, CC, CC), BF16),
            pltpu.VMEM((4 * CC, D), BF16),
            pltpu.VMEM((FREQ, 3 * D), F32),
            pltpu.VMEM((D, 3 * HD), BF16),
            pltpu.VMEM((8, HD, D), BF16),
            pltpu.VMEM((half, 128), F32),
            pltpu.VMEM((3, 6, 112, CC), F32),
            pltpu.VMEM((2, 6, 96, 128), F32),
            pltpu.VMEM((8, ROW, 4 * CC), BF16),
            pltpu.VMEM((ROW, D), BF16),
            pltpu.VMEM((3, D), F32),
            pltpu.VMEM((NTOK, HD), BF16),
            pltpu.VMEM((9, 2, NTOK, HD), BF16),
            pltpu.VMEM((NTOK, HD), F32),
            pltpu.VMEM((NTOK, HD), F32),
            pltpu.VMEM((NTOK, HD), F32),
            pltpu.VMEM((8, ROW, HD), BF16),
            pltpu.VMEM((8, ROW, HD), BF16),
            dma((9,)),
            dma((1,)),
            dma((5,)),
            dma((5,)),
            dma((7,)),
            dma((8,)),
            dma((4,)),
            dma((9, 2)),
            dma((8,)),
            dma((8,)),
            dma((8,)),
            dma((8,)),
            dma((8,)),
            dma((8,)),
        ],
        compiler_params=pltpu.CompilerParams(
            collective_id=0, has_side_effects=True, vmem_limit_bytes=56 * 1024 * 1024
        ),
        name="block",
    )(
        feats, conv_weight, conv_bias.reshape(1, CC), patch_weight, patch_bias.reshape(1, D), time_weight,
        qkv_weight, out_weight, steps_index, lookback, phi,
    )


def solution(mesh):
    in_specs = (
        P("tm", "height", None, None),
        P(),
        P(),
        P(),
        P(),
        P(),
        P(None, None, "height"),
        P("height", None),
        P("tm"),
        P("tm"),
    )
    out_specs = P("tm", "height", None, None)
    return jax.shard_map(
        on_device, mesh=mesh, in_specs=in_specs, out_specs=out_specs, check_vma=False
    )
```

```python
import math

import jax
import jax.numpy as jnp
from jax import lax
from jax.experimental import pallas as pl
from jax.experimental.pallas import tpu as pltpu
from jax.sharding import PartitionSpec as P

HD = 128
WIN = 8
D = 1536
CC = 192
FREQ = 256
ROW = 144
PIECE = 2 * ROW
HALF = 4 * ROW
NTOK = 8 * ROW
NEG = -1e30
MESH = pl.DeviceIdType.MESH
F32 = jnp.float32
BF16 = jnp.bfloat16


def kernel(
    feats, conv_w, conv_b, patch_w, patch_b, time_w, qkv_w, out_w, steps, lookback,
    out,
    own_rows, got_rows, fp, cw, pw, tw, wq, wo, ow, conv_acc, act, pat, tok, mod, q_ref, q_cols, kv, kv_far, acc, col_max, col_sum, obuf, mix,
    load_sem, z_send, z_recv, halo_send, halo_recv, pat_send, pat_recv, win_send, win_recv, fwd_send, mate_send,
    wo_sem, far_send, ow_send, ow_recv, share_send, share_recv, mix_send, mix_recv,
):
    tm = lax.axis_index("tm")
    h = lax.axis_index("height")
    x = tm // 8
    zl = (tm // 2) % 4
    c = tm % 2
    y = h // 2
    zh = h % 2

    def dev(x_, zl_, c_, y_, zh_):
        return (x_ * 8 + zl_ * 2 + c_, y_ * 2 + zh_)

    def remote(src, dst, send, recv, to):
        return pltpu.make_async_remote_copy(
            src_ref=src, dst_ref=dst, send_sem=send, recv_sem=recv, device_id=to, device_id_type=MESH
        )

    mine, theirs = 1 + 2 * zh, 3 - 2 * zh
    loads = [
        pltpu.make_async_copy(feats, fp.at[pl.ds(2, 3), pl.ds(mine, 2)], load_sem.at[0]),
        pltpu.make_async_copy(conv_w, cw, load_sem.at[1]),
        pltpu.make_async_copy(patch_w, pw, load_sem.at[2]),
        pltpu.make_async_copy(time_w, tw, load_sem.at[3]),
    ]
    for part in range(3):
        loads.append(
            pltpu.make_async_copy(qkv_w.at[part], wq.at[:, pl.ds(part * HD, HD)], load_sem.at[4 + part])
        )
    loads.append(pltpu.make_async_copy(out_w, ow.at[h], load_sem.at[7]))
    for cp in loads:
        cp.start()

    tm_next, tm_prev = (tm + 1) % 32, (tm + 31) % 32
    h_up, h_down = ((y + 1) % 4) * 2 + zh, ((y + 3) % 4) * 2 + zh
    partners = [(tm, (h + k) % 8) for k in range(1, 8)]
    partners += [(t, r) for t in (tm_next, tm_prev) for r in (h_down, h, h_up)]
    partners += [dev(x, (zl + k) % 4, c, y, zh) for k in (1, 3)]
    partners += [dev((x + k) % 4, zl, c, y, zh) for k in (1, 3)]
    partners += [dev(x, zl, 1 - c, y, zh)]
    partners += [dev(x, (zl + k) % 4, c, y, 1 - zh) for k in (1, 2, 3)]
    partners += [dev((x + k) % 4, 3 - zl, c, y, 1 - zh) for k in (1, 3)]
    barrier = pltpu.get_barrier_semaphore()
    for to in partners:
        pl.semaphore_signal(barrier, inc=1, device_id=to, device_id_type=MESH)

    loads[0].wait()
    for f in range(3):
        own_rows[f] = jnp.concatenate([fp[2 + f, mine], fp[2 + f, mine + 1]], axis=1)
    pl.semaphore_wait(barrier, len(partners))

    z_copies = {
        f: remote(own_rows.at[f], got_rows.at[f], z_send.at[f], z_recv.at[f], (tm, y * 2 + 1 - zh)) for f in (1, 2, 0)
    }
    for cp in z_copies.values():
        cp.start()

    def passing(rows, edge, to_up, first):
        to_h = to_up * h_up + (1 - to_up) * h_down
        at = 5 * (1 - to_up)
        late = fp.at[pl.ds(3, 2), pl.ds(edge, 1)]
        return [
            remote(
                fp.at[pl.ds(3, 2), pl.ds(rows, 2)], fp.at[pl.ds(0, 2), pl.ds(rows, 2)],
                halo_send.at[first], halo_recv.at[rows // 2], (tm_next, h),
            ),
            remote(late, fp.at[pl.ds(0, 2), pl.ds(at, 1)], halo_send.at[first + 1], halo_recv.at[2 + to_up], (tm_next, to_h)),
            remote(
                fp.at[pl.ds(2, 3), pl.ds(edge, 1)], fp.at[pl.ds(2, 3), pl.ds(at, 1)],
                halo_send.at[first + 2], halo_recv.at[4 + to_up], (tm, to_h),
            ),
        ]

    halo = passing(mine, 1 + 3 * zh, zh, 0)
    for cp in halo:
        cp.start()

    index = lax.broadcasted_iota(jnp.int32, (FREQ // 2, 128), 0)
    coarse = jnp.zeros((FREQ // 2, 128), F32)
    fine = jnp.zeros((FREQ // 2, 128), F32)
    for i in range(16):
        coarse = jnp.where(index // 8 == i, math.exp(-math.log(10000.0) * i / 16), coarse)
    for i in range(8):
        fine = jnp.where(index % 8 == i, math.exp(-math.log(10000.0) * i / 128), fine)
    angle = steps[0].astype(F32) * (coarse * fine)
    embedding = jnp.concatenate([jnp.cos(angle), jnp.sin(angle)], axis=0)
    loads[3].wait()
    for part in range(3):
        for tile in range(D // 128):
            lane = part * D + tile * 128
            mod[part : part + 1, tile * 128 : (tile + 1) * 128] = jnp.sum(
                tw[:, lane : lane + 128] * embedding, axis=0, keepdims=True
            )

    conv_acc[...] = jnp.zeros_like(conv_acc)
    loads[1].wait()
    for f, cp in z_copies.items():
        cp.wait_recv()
        both = got_rows[f]
        fp[2 + f, theirs] = both[:, :CC]
        fp[2 + f, theirs + 1] = both[:, CC:]
    halo_more = passing(theirs, 1 + 3 * (1 - zh), 1 - zh, 3)
    for cp in halo_more:
        cp.start()

    at_end = (zl % 3) == 0
    ow_near = dev(x, 3 * (1 - zl // 3), c, y, 1 - zh)
    ow_far = dev(x, 1 + (1 - zl // 3), c, y, 1 - zh)
    for cp in loads[4:7]:
        cp.wait()
    wo_copy = remote(wq.at[:, pl.ds(HD, 2 * HD)], wo, wo_sem.at[0], wo_sem.at[1], ow_near)

    @pl.when(at_end)
    def _():
        wo_copy.start()

    def tap(a, b, f, nf, r, nr):
        rows = fp[f + a : f + a + nf, r + b : r + b + nr].reshape(nf * nr * 96, CC)
        for e in range(3):
            term = jnp.dot(rows, cw[a, b, e], preferred_element_type=F32)
            conv_acc[e, f : f + nf, r : r + nr, 8:104] += term.reshape(nf, nr, 96, CC)

    for a in range(3):
        for b in range(3):
            tap(a, b, 2 - a, 1 + a, 1 if b == 0 else 0, 4 if b == 1 else 3)

    def halo_wait(f, nf, r, nr, sem):
        spot = fp.at[pl.ds(f, nf), pl.ds(r, nr)]
        remote(spot, spot, halo_send.at[0], halo_recv.at[sem], (tm_next, h)).wait_recv()

    halo_wait(0, 2, 1, 2, 0)
    halo_wait(0, 2, 3, 2, 1)
    halo_wait(0, 2, 5, 1, 2)
    halo_wait(0, 2, 0, 1, 3)
    halo_wait(2, 3, 5, 1, 4)
    halo_wait(2, 3, 0, 1, 5)

    @pl.when(y == 0)
    def _():
        fp[:, 0:1] = jnp.zeros((5, 1, 96, CC), BF16)

    @pl.when(y == 3)
    def _():
        fp[:, 5:6] = jnp.zeros((5, 1, 96, CC), BF16)

    @pl.when(tm == 0)
    def _():
        fp[0:2] = jnp.zeros((2, 6, 96, CC), BF16)

    for a in range(3):
        for b in range(3):
            if a < 2:
                tap(a, b, 0, 2 - a, 0, 4)
            if b != 1:
                tap(a, b, 2 - a, 1 + a, 0 if b == 0 else 3, 1)
    for f in range(3):
        for r in range(4):
            v = conv_acc[0, f, r, 7:103] + conv_acc[1, f, r, 8:104] + conv_acc[2, f, r, 9:105] + conv_b[...]
            v = v / (1.0 + jnp.exp(-v))
            act[0, f, r] = v[:, 0:128]
            act[1, f, r, :, 0:64] = v[:, 128:192]
    for f in range(3):
        for row in range(2):
            pieces = []
            for u in range(2):
                for w in range(2):
                    columns = pl.ds(w, 48, stride=2)
                    r = 2 * row + u
                    pieces += [act[0, f, r, columns, :], act[1, f, r, columns, :][:, :64]]
            pat[row, pl.ds(48 * f, 48)] = jnp.concatenate(pieces, axis=1).astype(BF16)

    def pat_copy(src, dst, sem, to):
        return remote(pat.at[src], pat.at[dst], pat_send.at[sem], pat_recv.at[dst], (tm, to))

    pat_copies = [
        pat_copy(0, 2, 0, h_up),
        pat_copy(1, 3, 1, h_down),
        pat_copy(1, 4, 2, h_up),
        pat_copy(0, 5, 3, h_down),
    ]
    pat_onward = [pat_copy(2, 6, 4, h_up), pat_copy(3, 7, 5, h_down)]
    order = [(0, 0), (0, 1), (3, 0), (1, 1), (3, 1), (1, 0), (2, 0), (2, 1)]
    for cp in pat_copies:
        cp.start()
    loads[2].wait()

    @pl.when(at_end)
    def _():
        wo_copy.wait_recv()

    def pat_wait(slot):
        remote(pat.at[slot], pat.at[slot], pat_send.at[0], pat_recv.at[slot], (tm, h_up)).wait_recv()

    own_part = pl.ds(pl.multiple_of(c * (HD // 2), HD // 2), HD // 2)
    ow_z = [
        remote(ow.at[h, own_part], ow.at[h, own_part], ow_send.at[6 + i], ow_recv.at[h], to)
        for i, to in enumerate((ow_near, ow_far))
    ]
    loads[7].wait()

    shift_row = mod[0:1, :]
    scale_row = 1.0 + mod[1:2, :]
    q_scale = HD ** (-0.5) * math.log2(math.e)

    def project(group):
        patches = pat[2 * group : 2 * group + 2].reshape(PIECE, 4 * CC)
        tokens = (jnp.dot(patches, pw[...], preferred_element_type=F32) + patch_b[...]).astype(BF16)
        if group == 0:

            @pl.when(zh == 0)
            def _():
                tok[...] = tokens[:ROW]

            @pl.when(zh == 1)
            def _():
                tok[...] = tokens[ROW:]

        wide = tokens.astype(F32)
        centered = wide - jnp.mean(wide, axis=-1, keepdims=True)
        variance = jnp.mean(centered * centered, axis=-1, keepdims=True)
        normed = (centered * lax.rsqrt(variance + 1e-06) * scale_row + shift_row).astype(BF16)
        qkv = jnp.dot(normed, wq[...], preferred_element_type=F32)
        rows = pl.ds(group * PIECE, PIECE)
        q_ref[rows, :] = (qkv[:, 0:HD] * q_scale).astype(BF16)
        kv[0, 0, rows, :] = qkv[:, HD : 2 * HD].astype(BF16)
        kv[0, 1, rows, :] = qkv[:, 2 * HD :].astype(BF16)

        @pl.when(at_end)
        def _():
            other = jnp.dot(normed, wo[...], preferred_element_type=F32).astype(BF16)
            kv_far[0, rows, :] = other[:, :HD]
            kv_far[1, rows, :] = other[:, HD:]

    def half_rows(g):
        return pl.ds(pl.multiple_of(g * HALF, HALF), HALF)

    def half_of(slot, g):
        return kv.at[slot, :, half_rows(g), :]

    def piece_of(slot, p):
        return kv.at[slot, :, pl.ds(pl.multiple_of(p * PIECE, PIECE), PIECE), :]

    z_next = dev(x, (zl + 1) % 4, c, y, zh)
    z_prev = dev(x, (zl + 3) % 4, c, y, zh)
    x_next = dev((x + 1) % 4, zl, c, y, zh)
    mate = dev(x, zl, 1 - c, y, zh)

    win_copies = []
    end_to = dev((x + zl // 3) % 4, 3 * (1 - zl // 3), c, y, 1 - zh)
    end_slot = 3 - 2 * (zl // 3)

    def send_own(p):
        up = remote(piece_of(0, p), piece_of(1, p), win_send.at[p], win_recv.at[1, p], z_next)
        across = remote(piece_of(0, p), piece_of(4, p), win_send.at[4 + p], win_recv.at[4, p], x_next)
        far = remote(
            kv_far.at[:, pl.ds(p * PIECE, PIECE)], piece_of(end_slot, p), far_send.at[p], win_recv.at[end_slot, p], end_to
        )
        across.start()

        @pl.when(zl < 3)
        def _():
            up.start()

        @pl.when(at_end)
        def _():
            far.start()

        win_copies.append((up, across, far))

    def passing_on(d, p):
        up = remote(piece_of(d, p), piece_of((d + 1) % 5, p), fwd_send.at[d - 1, p], win_recv.at[(d + 1) % 5, p], z_next)
        down = remote(piece_of(d, p), piece_of(d - 1, p), fwd_send.at[d - 1, p], win_recv.at[d - 1, p], z_prev)
        middle = jnp.logical_and(zl > 0, zl < 3)
        goes_up = jnp.logical_and(d == 1, middle)
        goes_down = jnp.logical_or(jnp.logical_and(d == 4, zl > 0), jnp.logical_and(d == 3, middle))
        return up, down, goes_up, goes_down

    def pass_on(d, p):
        remote(piece_of(0, p), piece_of(d, p), fwd_send.at[0, 0], win_recv.at[d, p], mate).wait_recv()
        up, down, goes_up, goes_down = passing_on(d, p)

        @pl.when(goes_up)
        def _():
            up.start()

        @pl.when(goes_down)
        def _():
            down.start()

    def share_copy(d, g):
        src = c * d + (1 - c) * (d % 4)
        dst = 4 + c * d + (1 - c) * (d % 4 + 1)
        return remote(half_of(src, g), half_of(dst, g), mate_send.at[d - 1, g], win_recv.at[dst, g], mate)

    project(0)
    send_own(0)

    @pl.when(at_end)
    def _():
        for cp in ow_z:
            cp.start()

    pat_wait(2)
    pat_onward[0].start()
    pat_wait(3)
    pat_onward[1].start()
    project(1)
    send_own(1)
    pat_wait(4)
    pat_wait(5)
    project(2)
    send_own(2)
    for d in (1, 4, 3):
        pass_on(d, 0)
    pat_wait(6)
    pat_wait(7)
    project(3)
    send_own(3)
    for d in (1, 4, 3):
        pass_on(d, 1)
        share_copy(d, 0).start()

    def ow_sends(row, first):
        part = ow.at[row, own_part]
        return [
            remote(part, part, ow_send.at[first + k], ow_recv.at[row], (tm, ((y + k + 1) % 4) * 2 + zh)) for k in (0, 2, 1)
        ]

    def ow_wait(row):
        part = ow.at[row, own_part]
        remote(part, part, ow_send.at[0], ow_recv.at[row], (tm, h_up)).wait_recv()

    def ow_share(row):
        part = ow.at[row, own_part]
        return remote(part, part, share_send.at[row], share_recv.at[row], mate)

    h_other = y * 2 + 1 - zh
    ow_copies = ow_sends(h, 0) + ow_sends(h_other, 3)
    for cp in ow_copies[:3]:
        cp.start()
    others = [h_other] + [((y + k) % 4) * 2 + half for k in range(1, 4) for half in range(2)]

    q_cols[...] = q_ref[...].astype(F32).T.astype(BF16)
    acc[...] = jnp.zeros_like(acc)
    col_sum[...] = jnp.zeros_like(col_sum)
    col_max[...] = jnp.full_like(col_max, NEG)

    def attend(slot, g, back):
        penalty = jnp.where(back <= lookback[0], 0.0, 1e30)
        values = kv[slot, 1, half_rows(g), :].T
        scores = jnp.dot(kv[slot, 0, half_rows(g), :], q_cols[...], preferred_element_type=F32)
        old = col_max[...]
        new = jnp.maximum(old, jnp.max(scores, axis=0, keepdims=True) - penalty)
        probs = jnp.exp2(scores - (new + penalty))
        shrink = jnp.exp2(old - new)
        col_max[...] = new
        col_sum[...] = col_sum[...] * shrink + jnp.sum(probs, axis=0, keepdims=True)
        acc[...] = acc[...] * shrink + jnp.dot(values, probs.astype(BF16), preferred_element_type=F32)

    def own_half(g, _):
        attend(0, g, 0)
        return 0

    lax.fori_loop(0, 2, own_half, 0)

    arrivals = [(1, 0), (4, 0), (3, 0), (1, 1), (4, 1), (3, 1), (2, 0), (2, 1)]
    code = sum(((d - 1) * 2 + g) * 8**i for i, (d, g) in enumerate(arrivals))

    def arrive(digit):
        d, g = digit // 2 + 1, digit % 2
        for k in range(2):
            pass_on(d, 2 * g + k)
        share_copy(d, g).start()

    def event(i, code):
        digit = code % 8
        d, g = digit // 2 + 1, digit % 2

        @pl.when(i < 3)
        def _():
            arrive((code // 512) % 8)

        @pl.when(i >= 6)
        def _():
            arrive(digit)

        attend(d, g, 2 * d)
        got = 4 + (1 - c) * d + c * (d % 4 + 1)
        remote(half_of(0, g), half_of(got, g), mate_send.at[0, 0], win_recv.at[got, g], mate).wait_recv()
        attend(got, g, 2 * (got - 4) - 1)
        return code // 8

    code_late = lax.fori_loop(0, 3, event, code)
    ow_wait(h_other)
    for cp in ow_copies[3:]:
        cp.start()
    code_late = lax.fori_loop(3, 7, event, code_late)
    for row in others[1:]:
        ow_wait(row)
    for row in others:
        ow_share(row).start()
    lax.fori_loop(7, 8, event, code_late)

    def mix_copy(s):
        to = ((y + order[s][0]) % 4) * 2 + order[s][1]
        return to, remote(obuf.at[s], mix.at[h], mix_send.at[s], mix_recv.at[h], (tm, to))

    all_out = (acc[...] / col_sum[...]).T.astype(BF16)
    for s in range(8):
        heads_out = all_out[s * ROW : (s + 1) * ROW]
        obuf[s] = heads_out
        to, cp = mix_copy(s)

        @pl.when(to == h)
        def _(heads_out=heads_out):
            mix[h] = heads_out

        @pl.when(to != h)
        def _(cp=cp):
            cp.start()

    for row in others:
        part = ow.at[row, pl.ds(pl.multiple_of((1 - c) * (HD // 2), HD // 2), HD // 2)]
        remote(part, part, share_send.at[row], share_recv.at[row], mate).wait_recv()
    for k in range(1, 8):
        r = (h + k) % 8
        remote(obuf.at[0], mix.at[r], mix_send.at[0], mix_recv.at[r], (tm, h_up)).wait_recv()
    heads = jnp.concatenate([mix[i] for i in range(8)], axis=1)
    attended = jnp.dot(heads, ow[...].reshape(8 * HD, D), preferred_element_type=F32)
    refined = (tok[...].astype(F32) + mod[2:3, :] * attended).astype(BF16)
    out[...] = refined.reshape(3, 1, 48, D)

    for cp in halo + halo_more + list(z_copies.values()) + pat_copies + pat_onward + ow_copies:
        cp.wait_send()
    for row in others:
        ow_share(row).wait_send()

    @pl.when(at_end)
    def _():
        for cp in ow_z + [wo_copy] + [far for _, _, far in win_copies]:
            cp.wait_send()

    for up, across, _ in win_copies:
        across.wait_send()

        @pl.when(zl < 3)
        def _(up=up):
            up.wait_send()

    def drain(i, _):
        d = i // 4 + 1
        up, down, goes_up, goes_down = passing_on(d, i % 4)

        @pl.when(goes_up)
        def _():
            up.wait_send()

        @pl.when(goes_down)
        def _():
            down.wait_send()

        return 0

    lax.fori_loop(0, 16, drain, 0)
    for d in range(1, 5):
        for g in range(2):
            share_copy(d, g).wait_send()

    for s in range(8):
        to, cp = mix_copy(s)

        @pl.when(to != h)
        def _(cp=cp):
            cp.wait_send()


def on_device(
    feats, conv_weight, conv_bias, patch_weight, patch_bias, time_weight, qkv_weight, out_weight, steps_index, lookback
):
    vmem = pl.BlockSpec(memory_space=pltpu.VMEM)
    smem = pl.BlockSpec(memory_space=pltpu.SMEM)
    hbm = pl.BlockSpec(memory_space=pl.ANY)
    dma = pltpu.SemaphoreType.DMA
    return pl.pallas_call(
        kernel,
        out_shape=jax.ShapeDtypeStruct((3, 1, 48, D), BF16),
        in_specs=[hbm, hbm, vmem, hbm, vmem, hbm, hbm, hbm, smem, smem],
        out_specs=vmem,
        scratch_shapes=[
            pltpu.VMEM((3, 96, 2 * CC), BF16),
            pltpu.VMEM((3, 96, 2 * CC), BF16),
            pltpu.VMEM((5, 6, 96, CC), BF16),
            pltpu.VMEM((3, 3, 3, CC, CC), BF16),
            pltpu.VMEM((4 * CC, D), BF16),
            pltpu.VMEM((FREQ, 3 * D), F32),
            pltpu.VMEM((D, 3 * HD), BF16),
            pltpu.VMEM((D, 2 * HD), BF16),
            pltpu.VMEM((8, HD, D), BF16),
            pltpu.VMEM((3, 3, 4, 112, CC), F32),
            pltpu.VMEM((2, 3, 4, 96, 128), F32),
            pltpu.VMEM((8, ROW, 4 * CC), BF16),
            pltpu.VMEM((ROW, D), BF16),
            pltpu.VMEM((3, D), F32),
            pltpu.VMEM((NTOK, HD), BF16),
            pltpu.VMEM((HD, NTOK), BF16),
            pltpu.VMEM((9, 2, NTOK, HD), BF16),
            pltpu.VMEM((2, NTOK, HD), BF16),
            pltpu.VMEM((HD, NTOK), F32),
            pltpu.VMEM((1, NTOK), F32),
            pltpu.VMEM((1, NTOK), F32),
            pltpu.VMEM((8, ROW, HD), BF16),
            pltpu.VMEM((8, ROW, HD), BF16),
            dma((8,)),
            dma((3,)),
            dma((3,)),
            dma((6,)),
            dma((6,)),
            dma((6,)),
            dma((8,)),
            dma((8,)),
            dma((9, 4)),
            dma((4, 4)),
            dma((4, 2)),
            dma((2,)),
            dma((4,)),
            dma((8,)),
            dma((8,)),
            dma((8,)),
            dma((8,)),
            dma((8,)),
            dma((8,)),
        ],
        compiler_params=pltpu.CompilerParams(
            collective_id=0, has_side_effects=True, vmem_limit_bytes=56 * 1024 * 1024
        ),
        name="block",
    )(
        feats, conv_weight, conv_bias, patch_weight, patch_bias, time_weight,
        qkv_weight, out_weight, steps_index, lookback,
    )


def solution(mesh):
    in_specs = (
        P("tm", "height", None, None),
        P(),
        P(),
        P(),
        P(),
        P(),
        P(None, None, "height"),
        P("height", None),
        P("tm"),
        P("tm"),
    )
    out_specs = P("tm", "height", None, None)
    return jax.shard_map(
        on_device, mesh=mesh, in_specs=in_specs, out_specs=out_specs, check_vma=False
    )
```

```python
import math

import jax
import jax.numpy as jnp
from jax import lax
from jax.experimental import pallas as pl
from jax.experimental.pallas import tpu as pltpu
from jax.sharding import PartitionSpec as P

HD = 128
WIN = 8
D = 1536
CC = 192
FREQ = 256
ROW = 144
PIECE = 2 * ROW
HALF = 4 * ROW
NTOK = 8 * ROW
NEG = -1e30
MESH = pl.DeviceIdType.MESH
F32 = jnp.float32
BF16 = jnp.bfloat16


def kernel(
    feats, conv_w, conv_b, patch_w, patch_b, time_w, qkv_w, out_w, steps, lookback,
    out,
    own_rows, got_rows, fp, cw, pw, tw, wq, wo, ow, conv_acc, act, pat, tok, mod, q_ref, q_cols, kv, kv_far, acc, col_max, col_sum, obuf, mix,
    load_sem, z_send, z_recv, halo_send, halo_recv, pat_send, pat_recv, win_send, win_recv, fwd_send, mate_send,
    wo_sem, far_send, ow_send, ow_recv, share_send, share_recv, mix_send, mix_recv,
):
    tm = lax.axis_index("tm")
    h = lax.axis_index("height")
    x = tm // 8
    zl = (tm // 2) % 4
    c = tm % 2
    y = h // 2
    zh = h % 2

    def dev(x_, zl_, c_, y_, zh_):
        return (x_ * 8 + zl_ * 2 + c_, y_ * 2 + zh_)

    def remote(src, dst, send, recv, to):
        return pltpu.make_async_remote_copy(
            src_ref=src, dst_ref=dst, send_sem=send, recv_sem=recv, device_id=to, device_id_type=MESH
        )

    mine, theirs = 1 + 2 * zh, 3 - 2 * zh
    loads = [
        pltpu.make_async_copy(feats, fp.at[pl.ds(2, 3), pl.ds(mine, 2)], load_sem.at[0]),
        pltpu.make_async_copy(conv_w, cw, load_sem.at[1]),
        pltpu.make_async_copy(patch_w, pw, load_sem.at[2]),
        pltpu.make_async_copy(time_w, tw, load_sem.at[3]),
    ]
    for part in range(3):
        loads.append(
            pltpu.make_async_copy(qkv_w.at[part], wq.at[:, pl.ds(part * HD, HD)], load_sem.at[4 + part])
        )
    loads.append(pltpu.make_async_copy(out_w, ow.at[h], load_sem.at[7]))
    for cp in loads:
        cp.start()

    tm_next, tm_prev = (tm + 1) % 32, (tm + 31) % 32
    h_up, h_down = ((y + 1) % 4) * 2 + zh, ((y + 3) % 4) * 2 + zh
    partners = [(tm, (h + k) % 8) for k in range(1, 8)]
    partners += [(t, r) for t in (tm_next, tm_prev) for r in (h_down, h, h_up)]
    partners += [dev(x, (zl + k) % 4, c, y, zh) for k in (1, 3)]
    partners += [dev((x + k) % 4, zl, c, y, zh) for k in (1, 3)]
    partners += [dev(x, zl, 1 - c, y, zh)]
    partners += [dev(x, (zl + k) % 4, c, y, 1 - zh) for k in (1, 2, 3)]
    partners += [dev((x + k) % 4, 3 - zl, c, y, 1 - zh) for k in (1, 3)]
    barrier = pltpu.get_barrier_semaphore()
    for to in partners:
        pl.semaphore_signal(barrier, inc=1, device_id=to, device_id_type=MESH)

    loads[0].wait()
    for f in range(3):
        own_rows[f] = jnp.concatenate([fp[2 + f, mine], fp[2 + f, mine + 1]], axis=1)
    pl.semaphore_wait(barrier, len(partners))

    z_copies = {
        f: remote(own_rows.at[f], got_rows.at[f], z_send.at[f], z_recv.at[f], (tm, y * 2 + 1 - zh)) for f in (1, 2, 0)
    }
    for cp in z_copies.values():
        cp.start()

    def passing(rows, edge, to_up, first):
        to_h = to_up * h_up + (1 - to_up) * h_down
        at = 5 * (1 - to_up)
        late = fp.at[pl.ds(3, 2), pl.ds(edge, 1)]
        return [
            remote(
                fp.at[pl.ds(3, 2), pl.ds(rows, 2)], fp.at[pl.ds(0, 2), pl.ds(rows, 2)],
                halo_send.at[first], halo_recv.at[rows // 2], (tm_next, h),
            ),
            remote(late, fp.at[pl.ds(0, 2), pl.ds(at, 1)], halo_send.at[first + 1], halo_recv.at[2 + to_up], (tm_next, to_h)),
            remote(
                fp.at[pl.ds(2, 3), pl.ds(edge, 1)], fp.at[pl.ds(2, 3), pl.ds(at, 1)],
                halo_send.at[first + 2], halo_recv.at[4 + to_up], (tm, to_h),
            ),
        ]

    halo = passing(mine, 1 + 3 * zh, zh, 0)
    for cp in halo:
        cp.start()

    index = lax.broadcasted_iota(jnp.int32, (FREQ // 2, 128), 0)
    coarse = jnp.zeros((FREQ // 2, 128), F32)
    fine = jnp.zeros((FREQ // 2, 128), F32)
    for i in range(16):
        coarse = jnp.where(index // 8 == i, math.exp(-math.log(10000.0) * i / 16), coarse)
    for i in range(8):
        fine = jnp.where(index % 8 == i, math.exp(-math.log(10000.0) * i / 128), fine)
    angle = steps[0].astype(F32) * (coarse * fine)
    embedding = jnp.concatenate([jnp.cos(angle), jnp.sin(angle)], axis=0)
    loads[3].wait()
    for part in range(3):
        for tile in range(D // 128):
            lane = part * D + tile * 128
            mod[part : part + 1, tile * 128 : (tile + 1) * 128] = jnp.sum(
                tw[:, lane : lane + 128] * embedding, axis=0, keepdims=True
            )

    conv_acc[...] = jnp.zeros_like(conv_acc)
    loads[1].wait()
    halo_more = passing(theirs, 1 + 3 * (1 - zh), 1 - zh, 3)
    for f, cp in z_copies.items():
        cp.wait_recv()
        both = got_rows[f]
        fp[2 + f, theirs] = both[:, :CC]
        fp[2 + f, theirs + 1] = both[:, CC:]
        if f == 2:
            halo_more[0].start()
            halo_more[1].start()
    halo_more[2].start()

    at_end = (zl % 3) == 0
    ow_near = dev(x, 3 * (1 - zl // 3), c, y, 1 - zh)
    ow_far = dev(x, 1 + (1 - zl // 3), c, y, 1 - zh)
    for cp in loads[4:7]:
        cp.wait()
    wo_rows = pl.ds(pl.multiple_of(c * (D // 2), D // 2), D // 2)
    wo_rest = pl.ds(pl.multiple_of((1 - c) * (D // 2), D // 2), D // 2)
    wo_copy = remote(wq.at[wo_rows, pl.ds(HD, 2 * HD)], wo.at[wo_rows], wo_sem.at[0], wo_sem.at[1], ow_near)
    wo_share = remote(wo.at[wo_rows], wo.at[wo_rows], wo_sem.at[2], wo_sem.at[3], dev(x, zl, 1 - c, y, zh))

    @pl.when(at_end)
    def _():
        wo_copy.start()

    def tap(a, b, f, nf, r, nr):
        rows = fp[f + a : f + a + nf, r + b : r + b + nr].reshape(nf * nr * 96, CC)
        for e in range(3):
            term = jnp.dot(rows, cw[a, b, e], preferred_element_type=F32)
            conv_acc[e, f : f + nf, r : r + nr, 8:104] += term.reshape(nf, nr, 96, CC)

    for a in range(3):
        for b in range(3):
            tap(a, b, 2 - a, 1 + a, 1 if b == 0 else 0, 4 if b == 1 else 3)

    def halo_wait(f, nf, r, nr, sem):
        spot = fp.at[pl.ds(f, nf), pl.ds(r, nr)]
        remote(spot, spot, halo_send.at[0], halo_recv.at[sem], (tm_next, h)).wait_recv()

    halo_wait(0, 2, 1, 2, 0)
    halo_wait(0, 2, 3, 2, 1)
    halo_wait(0, 2, 5, 1, 2)
    halo_wait(0, 2, 0, 1, 3)
    halo_wait(2, 3, 5, 1, 4)
    halo_wait(2, 3, 0, 1, 5)

    @pl.when(y == 0)
    def _():
        fp[:, 0:1] = jnp.zeros((5, 1, 96, CC), BF16)

    @pl.when(y == 3)
    def _():
        fp[:, 5:6] = jnp.zeros((5, 1, 96, CC), BF16)

    @pl.when(tm == 0)
    def _():
        fp[0:2] = jnp.zeros((2, 6, 96, CC), BF16)

    for a in range(3):
        for b in range(3):
            if a < 2:
                tap(a, b, 0, 2 - a, 0, 4)
            if b != 1:
                tap(a, b, 2 - a, 1 + a, 0 if b == 0 else 3, 1)
    for f in range(3):
        for r in range(4):
            v = conv_acc[0, f, r, 7:103] + conv_acc[1, f, r, 8:104] + conv_acc[2, f, r, 9:105] + conv_b[...]
            v = v / (1.0 + jnp.exp(-v))
            act[0, f, r] = v[:, 0:128]
            act[1, f, r, :, 0:64] = v[:, 128:192]
    for f in range(3):
        for row in range(2):
            pieces = []
            for u in range(2):
                for w in range(2):
                    columns = pl.ds(w, 48, stride=2)
                    r = 2 * row + u
                    pieces += [act[0, f, r, columns, :], act[1, f, r, columns, :][:, :64]]
            pat[row, pl.ds(48 * f, 48)] = jnp.concatenate(pieces, axis=1).astype(BF16)

    def pat_copy(src, dst, sem, to):
        return remote(pat.at[src], pat.at[dst], pat_send.at[sem], pat_recv.at[dst], (tm, to))

    pat_copies = [
        pat_copy(0, 2, 0, h_up),
        pat_copy(1, 3, 1, h_down),
        pat_copy(1, 4, 2, h_up),
        pat_copy(0, 5, 3, h_down),
    ]
    pat_onward = [pat_copy(2, 6, 4, h_up), pat_copy(3, 7, 5, h_down)]
    order = [(0, 0), (0, 1), (3, 0), (1, 1), (3, 1), (1, 0), (2, 0), (2, 1)]
    for cp in pat_copies:
        cp.start()
    loads[2].wait()

    @pl.when(at_end)
    def _():
        wo_copy.wait_recv()
        wo_share.start()
        remote(wo.at[wo_rest], wo.at[wo_rest], wo_sem.at[2], wo_sem.at[3], dev(x, zl, 1 - c, y, zh)).wait_recv()

    def pat_wait(slot):
        remote(pat.at[slot], pat.at[slot], pat_send.at[0], pat_recv.at[slot], (tm, h_up)).wait_recv()

    own_part = pl.ds(pl.multiple_of(c * (HD // 2), HD // 2), HD // 2)
    ow_z = [
        remote(ow.at[h, own_part], ow.at[h, own_part], ow_send.at[6 + i], ow_recv.at[h], to)
        for i, to in enumerate((ow_near, ow_far))
    ]
    loads[7].wait()

    shift_row = mod[0:1, :]
    scale_row = 1.0 + mod[1:2, :]
    q_scale = HD ** (-0.5) * math.log2(math.e)

    def project(group):
        patches = pat[2 * group : 2 * group + 2].reshape(PIECE, 4 * CC)
        tokens = (jnp.dot(patches, pw[...], preferred_element_type=F32) + patch_b[...]).astype(BF16)
        if group == 0:

            @pl.when(zh == 0)
            def _():
                tok[...] = tokens[:ROW]

            @pl.when(zh == 1)
            def _():
                tok[...] = tokens[ROW:]

        wide = tokens.astype(F32)
        centered = wide - jnp.mean(wide, axis=-1, keepdims=True)
        variance = jnp.mean(centered * centered, axis=-1, keepdims=True)
        normed = (centered * lax.rsqrt(variance + 1e-06) * scale_row + shift_row).astype(BF16)
        qkv = jnp.dot(normed, wq[...], preferred_element_type=F32)
        rows = pl.ds(group * PIECE, PIECE)
        q_ref[rows, :] = (qkv[:, 0:HD] * q_scale).astype(BF16)
        kv[0, 0, rows, :] = qkv[:, HD : 2 * HD].astype(BF16)
        kv[0, 1, rows, :] = qkv[:, 2 * HD :].astype(BF16)

        @pl.when(at_end)
        def _():
            other = jnp.dot(normed, wo[...], preferred_element_type=F32).astype(BF16)
            kv_far[0, rows, :] = other[:, :HD]
            kv_far[1, rows, :] = other[:, HD:]

    def half_rows(g):
        return pl.ds(pl.multiple_of(g * HALF, HALF), HALF)

    def half_of(slot, g):
        return kv.at[slot, :, half_rows(g), :]

    def piece_of(slot, p):
        return kv.at[slot, :, pl.ds(pl.multiple_of(p * PIECE, PIECE), PIECE), :]

    z_next = dev(x, (zl + 1) % 4, c, y, zh)
    z_prev = dev(x, (zl + 3) % 4, c, y, zh)
    x_next = dev((x + 1) % 4, zl, c, y, zh)
    mate = dev(x, zl, 1 - c, y, zh)

    win_copies = []
    end_to = dev((x + zl // 3) % 4, 3 * (1 - zl // 3), c, y, 1 - zh)
    end_slot = 3 - 2 * (zl // 3)

    def send_own(p):
        up = remote(piece_of(0, p), piece_of(1, p), win_send.at[p], win_recv.at[1, p], z_next)
        across = remote(piece_of(0, p), piece_of(4, p), win_send.at[4 + p], win_recv.at[4, p], x_next)
        far = remote(
            kv_far.at[:, pl.ds(p * PIECE, PIECE)], piece_of(end_slot, p), far_send.at[p], win_recv.at[end_slot, p], end_to
        )
        across.start()

        @pl.when(zl < 3)
        def _():
            up.start()

        @pl.when(at_end)
        def _():
            far.start()

        win_copies.append((up, across, far))

    def passing_on(d, p):
        up = remote(piece_of(d, p), piece_of((d + 1) % 5, p), fwd_send.at[d - 1, p], win_recv.at[(d + 1) % 5, p], z_next)
        down = remote(piece_of(d, p), piece_of(d - 1, p), fwd_send.at[d - 1, p], win_recv.at[d - 1, p], z_prev)
        middle = jnp.logical_and(zl > 0, zl < 3)
        goes_up = jnp.logical_and(d == 1, middle)
        goes_down = jnp.logical_or(jnp.logical_and(d == 4, zl > 0), jnp.logical_and(d == 3, middle))
        return up, down, goes_up, goes_down

    def pass_on(d, p):
        remote(piece_of(0, p), piece_of(d, p), fwd_send.at[0, 0], win_recv.at[d, p], mate).wait_recv()
        up, down, goes_up, goes_down = passing_on(d, p)

        @pl.when(goes_up)
        def _():
            up.start()

        @pl.when(goes_down)
        def _():
            down.start()

    def share_copy(d, g):
        src = c * d + (1 - c) * (d % 4)
        dst = 4 + c * d + (1 - c) * (d % 4 + 1)
        return remote(half_of(src, g), half_of(dst, g), mate_send.at[d - 1, g], win_recv.at[dst, g], mate)

    project(0)
    send_own(0)

    @pl.when(at_end)
    def _():
        for cp in ow_z:
            cp.start()

    pat_wait(2)
    pat_onward[0].start()
    pat_wait(3)
    pat_onward[1].start()
    project(1)
    send_own(1)
    pat_wait(4)
    pat_wait(5)
    project(2)
    send_own(2)
    for d in (1, 4):
        pass_on(d, 0)
    pat_wait(6)
    pat_wait(7)
    project(3)
    send_own(3)
    for d in (1, 4):
        pass_on(d, 1)
        share_copy(d, 0).start()
    pass_on(3, 0)

    def ow_sends(row, first):
        part = ow.at[row, own_part]
        return [
            remote(part, part, ow_send.at[first + k], ow_recv.at[row], (tm, ((y + k + 1) % 4) * 2 + zh)) for k in (0, 2, 1)
        ]

    def ow_wait(row):
        part = ow.at[row, own_part]
        remote(part, part, ow_send.at[0], ow_recv.at[row], (tm, h_up)).wait_recv()

    def ow_share(row):
        part = ow.at[row, own_part]
        return remote(part, part, share_send.at[row], share_recv.at[row], mate)

    h_other = y * 2 + 1 - zh
    ow_copies = ow_sends(h, 0) + ow_sends(h_other, 3)
    for cp in ow_copies[:3]:
        cp.start()
    others = [h_other] + [((y + k) % 4) * 2 + half for k in range(1, 4) for half in range(2)]

    q_cols[...] = q_ref[...].astype(F32).T.astype(BF16)
    acc[...] = jnp.zeros_like(acc)
    col_sum[...] = jnp.zeros_like(col_sum)
    col_max[...] = jnp.full_like(col_max, NEG)

    def attend(slot, g, back):
        penalty = jnp.where(back <= lookback[0], 0.0, 1e30)
        values = kv[slot, 1, half_rows(g), :].T
        scores = jnp.dot(kv[slot, 0, half_rows(g), :], q_cols[...], preferred_element_type=F32)
        old = col_max[...]
        new = jnp.maximum(old, jnp.max(scores, axis=0, keepdims=True) - penalty)
        probs = jnp.exp2(scores - (new + penalty))
        shrink = jnp.exp2(old - new)
        col_max[...] = new
        col_sum[...] = col_sum[...] * shrink + jnp.sum(probs, axis=0, keepdims=True)
        acc[...] = acc[...] * shrink + jnp.dot(values, probs.astype(BF16), preferred_element_type=F32)

    arrivals = [(1, 0), (4, 0), (3, 0), (1, 1), (4, 1), (3, 1), (2, 0), (2, 1)]
    code = sum(((d - 1) * 2 + g) * 8**i for i, (d, g) in enumerate(arrivals))
    steps_of = {
        0: ([(1, 2), (4, 2)], []),
        1: ([(3, 1), (1, 3), (4, 3)], [(3, 0), (1, 1), (4, 1)]),
        2: ([(3, 2)], []),
        3: ([(3, 3)], [(3, 1)]),
        4: ([(2, 0), (2, 1)], [(2, 0)]),
        6: ([(2, 2), (2, 3)], [(2, 1)]),
    }

    def event(n, code):
        for at, (passed, shared) in steps_of.items():

            @pl.when(n == at)
            def _(passed=passed, shared=shared):
                for d, p in passed:
                    pass_on(d, p)
                for d, g in shared:
                    share_copy(d, g).start()

        @pl.when(n == 3)
        def _():
            ow_wait(h_other)
            for cp in ow_copies[3:]:
                cp.start()

        @pl.when(n == 7)
        def _():
            for row in others[1:]:
                ow_wait(row)
            for row in others:
                ow_share(row).start()

        first = (8 - n) // 8
        digit = code % 8
        d = (1 - first) * (digit // 2 + 1)
        g = (1 - first) * (digit % 2)
        got = 4 + (1 - c) * d + c * (d % 4 + 1)

        def one(k, _):
            @pl.when(jnp.logical_and(n > 0, k == 1))
            def _():
                remote(half_of(0, g), half_of(got, g), mate_send.at[0, 0], win_recv.at[got, g], mate).wait_recv()

            slot = (1 - k) * d + k * (1 - first) * got
            back = jnp.where(slot <= 4, 2 * slot, 2 * slot - 9)
            attend(slot, g + k * first, back)
            return 0

        lax.fori_loop(0, 2, one, 0)
        return first * code + (1 - first) * (code // 8)

    lax.fori_loop(0, 9, event, code)

    def mix_copy(s):
        to = ((y + order[s][0]) % 4) * 2 + order[s][1]
        return to, remote(obuf.at[s], mix.at[h], mix_send.at[s], mix_recv.at[h], (tm, to))

    all_out = (acc[...] / col_sum[...]).T.astype(BF16)
    for s in range(8):
        heads_out = all_out[s * ROW : (s + 1) * ROW]
        obuf[s] = heads_out
        to, cp = mix_copy(s)

        @pl.when(to == h)
        def _(heads_out=heads_out):
            mix[h] = heads_out

        @pl.when(to != h)
        def _(cp=cp):
            cp.start()

    for row in others:
        part = ow.at[row, pl.ds(pl.multiple_of((1 - c) * (HD // 2), HD // 2), HD // 2)]
        remote(part, part, share_send.at[row], share_recv.at[row], mate).wait_recv()
    for k in range(1, 8):
        r = (h + k) % 8
        remote(obuf.at[0], mix.at[r], mix_send.at[0], mix_recv.at[r], (tm, h_up)).wait_recv()
    heads = jnp.concatenate([mix[i] for i in range(8)], axis=1)
    attended = jnp.dot(heads, ow[...].reshape(8 * HD, D), preferred_element_type=F32)
    refined = (tok[...].astype(F32) + mod[2:3, :] * attended).astype(BF16)
    out[...] = refined.reshape(3, 1, 48, D)

    for cp in halo + halo_more + list(z_copies.values()) + pat_copies + pat_onward + ow_copies:
        cp.wait_send()
    for row in others:
        ow_share(row).wait_send()

    @pl.when(at_end)
    def _():
        for cp in ow_z + [wo_copy, wo_share] + [far for _, _, far in win_copies]:
            cp.wait_send()

    for up, across, _ in win_copies:
        across.wait_send()

        @pl.when(zl < 3)
        def _(up=up):
            up.wait_send()

    def drain(i, _):
        d = i // 4 + 1
        up, down, goes_up, goes_down = passing_on(d, i % 4)

        @pl.when(goes_up)
        def _():
            up.wait_send()

        @pl.when(goes_down)
        def _():
            down.wait_send()

        return 0

    lax.fori_loop(0, 16, drain, 0)
    for d in range(1, 5):
        for g in range(2):
            share_copy(d, g).wait_send()

    for s in range(8):
        to, cp = mix_copy(s)

        @pl.when(to != h)
        def _(cp=cp):
            cp.wait_send()


def on_device(
    feats, conv_weight, conv_bias, patch_weight, patch_bias, time_weight, qkv_weight, out_weight, steps_index, lookback
):
    vmem = pl.BlockSpec(memory_space=pltpu.VMEM)
    smem = pl.BlockSpec(memory_space=pltpu.SMEM)
    hbm = pl.BlockSpec(memory_space=pl.ANY)
    dma = pltpu.SemaphoreType.DMA
    return pl.pallas_call(
        kernel,
        out_shape=jax.ShapeDtypeStruct((3, 1, 48, D), BF16),
        in_specs=[hbm, hbm, vmem, hbm, vmem, hbm, hbm, hbm, smem, smem],
        out_specs=vmem,
        scratch_shapes=[
            pltpu.VMEM((3, 96, 2 * CC), BF16),
            pltpu.VMEM((3, 96, 2 * CC), BF16),
            pltpu.VMEM((5, 6, 96, CC), BF16),
            pltpu.VMEM((3, 3, 3, CC, CC), BF16),
            pltpu.VMEM((4 * CC, D), BF16),
            pltpu.VMEM((FREQ, 3 * D), F32),
            pltpu.VMEM((D, 3 * HD), BF16),
            pltpu.VMEM((D, 2 * HD), BF16),
            pltpu.VMEM((8, HD, D), BF16),
            pltpu.VMEM((3, 3, 4, 112, CC), F32),
            pltpu.VMEM((2, 3, 4, 96, 128), F32),
            pltpu.VMEM((8, ROW, 4 * CC), BF16),
            pltpu.VMEM((ROW, D), BF16),
            pltpu.VMEM((3, D), F32),
            pltpu.VMEM((NTOK, HD), BF16),
            pltpu.VMEM((HD, NTOK), BF16),
            pltpu.VMEM((9, 2, NTOK, HD), BF16),
            pltpu.VMEM((2, NTOK, HD), BF16),
            pltpu.VMEM((HD, NTOK), F32),
            pltpu.VMEM((1, NTOK), F32),
            pltpu.VMEM((1, NTOK), F32),
            pltpu.VMEM((8, ROW, HD), BF16),
            pltpu.VMEM((8, ROW, HD), BF16),
            dma((8,)),
            dma((3,)),
            dma((3,)),
            dma((6,)),
            dma((6,)),
            dma((6,)),
            dma((8,)),
            dma((8,)),
            dma((9, 4)),
            dma((4, 4)),
            dma((4, 2)),
            dma((4,)),
            dma((4,)),
            dma((8,)),
            dma((8,)),
            dma((8,)),
            dma((8,)),
            dma((8,)),
            dma((8,)),
        ],
        compiler_params=pltpu.CompilerParams(
            collective_id=0, has_side_effects=True, vmem_limit_bytes=56 * 1024 * 1024
        ),
        name="block",
    )(
        feats, conv_weight, conv_bias, patch_weight, patch_bias, time_weight,
        qkv_weight, out_weight, steps_index, lookback,
    )


def solution(mesh):
    in_specs = (
        P("tm", "height", None, None),
        P(),
        P(),
        P(),
        P(),
        P(),
        P(None, None, "height"),
        P("height", None),
        P("tm"),
        P("tm"),
    )
    out_specs = P("tm", "height", None, None)
    return jax.shard_map(
        on_device, mesh=mesh, in_specs=in_specs, out_specs=out_specs, check_vma=False
    )
```

```python
import math

import jax
import jax.numpy as jnp
from jax import lax
from jax.experimental import pallas as pl
from jax.experimental.pallas import tpu as pltpu
from jax.sharding import PartitionSpec as P

HD = 128
WIN = 8
D = 1536
CC = 192
FREQ = 256
ROW = 144
PIECE = 2 * ROW
HALF = 4 * ROW
NTOK = 8 * ROW
NEG = -1e30
MESH = pl.DeviceIdType.MESH
F32 = jnp.float32
BF16 = jnp.bfloat16


def kernel(
    feats, conv_w, conv_b, patch_w, patch_b, time_w, qkv_w, out_w, steps, lookback,
    out,
    own_rows, got_rows, fp, cw, pw, tw, wq, wo, ow, conv_acc, act, pat, tok, mod, q_ref, q_cols, kv, kv_far, acc, col_max, col_sum, obuf, mix,
    load_sem, z_send, z_recv, halo_send, halo_recv, pat_send, pat_recv, win_send, win_recv, fwd_send, mate_send,
    wo_sem, far_send, ow_send, ow_recv, share_send, share_recv, mix_send, mix_recv,
):
    tm = lax.axis_index("tm")
    h = lax.axis_index("height")
    x = tm // 8
    zl = (tm // 2) % 4
    c = tm % 2
    y = h // 2
    zh = h % 2

    def dev(x_, zl_, c_, y_, zh_):
        return (x_ * 8 + zl_ * 2 + c_, y_ * 2 + zh_)

    def remote(src, dst, send, recv, to):
        return pltpu.make_async_remote_copy(
            src_ref=src, dst_ref=dst, send_sem=send, recv_sem=recv, device_id=to, device_id_type=MESH
        )

    mine, theirs = 1 + 2 * zh, 3 - 2 * zh
    loads = [
        pltpu.make_async_copy(feats, fp.at[pl.ds(2, 3), pl.ds(mine, 2)], load_sem.at[0]),
        pltpu.make_async_copy(conv_w, cw, load_sem.at[1]),
        pltpu.make_async_copy(patch_w, pw, load_sem.at[2]),
        pltpu.make_async_copy(time_w, tw, load_sem.at[3]),
    ]
    for part in range(3):
        loads.append(
            pltpu.make_async_copy(qkv_w.at[part], wq.at[:, pl.ds(part * HD, HD)], load_sem.at[4 + part])
        )
    loads.append(pltpu.make_async_copy(out_w, ow.at[h], load_sem.at[7]))
    for cp in loads:
        cp.start()

    tm_next, tm_prev = (tm + 1) % 32, (tm + 31) % 32
    h_up, h_down = ((y + 1) % 4) * 2 + zh, ((y + 3) % 4) * 2 + zh
    partners = [(tm, (h + k) % 8) for k in range(1, 8)]
    partners += [(t, r) for t in (tm_next, tm_prev) for r in (h_down, h, h_up)]
    partners += [dev(x, (zl + k) % 4, c, y, zh) for k in (1, 3)]
    partners += [dev((x + k) % 4, zl, c, y, zh) for k in (1, 3)]
    partners += [dev(x, zl, 1 - c, y, zh)]
    partners += [dev(x, (zl + k) % 4, c, y, 1 - zh) for k in (1, 2, 3)]
    partners += [dev((x + k) % 4, 3 - zl, c, y, 1 - zh) for k in (1, 3)]
    barrier = pltpu.get_barrier_semaphore()
    for to in partners:
        pl.semaphore_signal(barrier, inc=1, device_id=to, device_id_type=MESH)

    loads[0].wait()
    for f in range(3):
        own_rows[f] = jnp.concatenate([fp[2 + f, mine], fp[2 + f, mine + 1]], axis=1)
    pl.semaphore_wait(barrier, len(partners))

    z_copies = {
        f: remote(own_rows.at[f], got_rows.at[f], z_send.at[f], z_recv.at[f], (tm, y * 2 + 1 - zh)) for f in (1, 2, 0)
    }
    for cp in z_copies.values():
        cp.start()

    def passing(rows, edge, to_up, first):
        to_h = to_up * h_up + (1 - to_up) * h_down
        at = 5 * (1 - to_up)
        late = fp.at[pl.ds(3, 2), pl.ds(edge, 1)]
        return [
            remote(
                fp.at[pl.ds(3, 2), pl.ds(rows, 2)], fp.at[pl.ds(0, 2), pl.ds(rows, 2)],
                halo_send.at[first], halo_recv.at[rows // 2], (tm_next, h),
            ),
            remote(late, fp.at[pl.ds(0, 2), pl.ds(at, 1)], halo_send.at[first + 1], halo_recv.at[2 + to_up], (tm_next, to_h)),
            remote(
                fp.at[pl.ds(2, 3), pl.ds(edge, 1)], fp.at[pl.ds(2, 3), pl.ds(at, 1)],
                halo_send.at[first + 2], halo_recv.at[4 + to_up], (tm, to_h),
            ),
        ]

    halo = passing(mine, 1 + 3 * zh, zh, 0)
    for cp in halo:
        cp.start()

    index = lax.broadcasted_iota(jnp.int32, (FREQ // 2, 128), 0)
    coarse = jnp.zeros((FREQ // 2, 128), F32)
    fine = jnp.zeros((FREQ // 2, 128), F32)
    for i in range(16):
        coarse = jnp.where(index // 8 == i, math.exp(-math.log(10000.0) * i / 16), coarse)
    for i in range(8):
        fine = jnp.where(index % 8 == i, math.exp(-math.log(10000.0) * i / 128), fine)
    angle = steps[0].astype(F32) * (coarse * fine)
    embedding = jnp.concatenate([jnp.cos(angle), jnp.sin(angle)], axis=0)
    loads[3].wait()
    for part in range(3):
        for tile in range(D // 128):
            lane = part * D + tile * 128
            mod[part : part + 1, tile * 128 : (tile + 1) * 128] = jnp.sum(
                tw[:, lane : lane + 128] * embedding, axis=0, keepdims=True
            )

    conv_acc[...] = jnp.zeros_like(conv_acc)
    loads[1].wait()
    halo_more = passing(theirs, 1 + 3 * (1 - zh), 1 - zh, 3)
    for f, cp in z_copies.items():
        cp.wait_recv()
        both = got_rows[f]
        fp[2 + f, theirs] = both[:, :CC]
        fp[2 + f, theirs + 1] = both[:, CC:]
        if f == 2:
            halo_more[0].start()
            halo_more[1].start()
    halo_more[2].start()

    at_end = (zl % 3) == 0
    ow_near = dev(x, 3 * (1 - zl // 3), c, y, 1 - zh)
    ow_far = dev(x, 1 + (1 - zl // 3), c, y, 1 - zh)
    for cp in loads[4:7]:
        cp.wait()
    wo_rows = pl.ds(pl.multiple_of(c * (D // 2), D // 2), D // 2)
    wo_rest = pl.ds(pl.multiple_of((1 - c) * (D // 2), D // 2), D // 2)
    wo_copy = remote(wq.at[wo_rows, pl.ds(HD, 2 * HD)], wo.at[wo_rows], wo_sem.at[0], wo_sem.at[1], ow_near)
    wo_share = remote(wo.at[wo_rows], wo.at[wo_rows], wo_sem.at[2], wo_sem.at[3], dev(x, zl, 1 - c, y, zh))

    @pl.when(at_end)
    def _():
        wo_copy.start()

    def tap(a, b, f, nf, r, nr):
        rows = fp[f + a : f + a + nf, r + b : r + b + nr].reshape(nf * nr * 96, CC)
        for e in range(3):
            term = jnp.dot(rows, cw[a, b, e], preferred_element_type=F32)
            conv_acc[e, f : f + nf, r : r + nr, 8:104] += term.reshape(nf, nr, 96, CC)

    for a in range(3):
        for b in range(3):
            tap(a, b, 2 - a, 1 + a, 1 if b == 0 else 0, 4 if b == 1 else 3)

    def halo_wait(f, nf, r, nr, sem):
        spot = fp.at[pl.ds(f, nf), pl.ds(r, nr)]
        remote(spot, spot, halo_send.at[0], halo_recv.at[sem], (tm_next, h)).wait_recv()

    halo_wait(0, 2, 1, 2, 0)
    halo_wait(0, 2, 3, 2, 1)
    halo_wait(0, 2, 5, 1, 2)
    halo_wait(0, 2, 0, 1, 3)
    halo_wait(2, 3, 5, 1, 4)
    halo_wait(2, 3, 0, 1, 5)

    @pl.when(y == 0)
    def _():
        fp[:, 0:1] = jnp.zeros((5, 1, 96, CC), BF16)

    @pl.when(y == 3)
    def _():
        fp[:, 5:6] = jnp.zeros((5, 1, 96, CC), BF16)

    @pl.when(tm == 0)
    def _():
        fp[0:2] = jnp.zeros((2, 6, 96, CC), BF16)

    for a in range(3):
        for b in range(3):
            if a < 2:
                tap(a, b, 0, 2 - a, 0, 4)
            if b != 1:
                tap(a, b, 2 - a, 1 + a, 0 if b == 0 else 3, 1)
    for f in range(3):
        for r in range(4):
            v = conv_acc[0, f, r, 7:103] + conv_acc[1, f, r, 8:104] + conv_acc[2, f, r, 9:105] + conv_b[...]
            v = v / (1.0 + jnp.exp(-v))
            act[0, f, r] = v[:, 0:128]
            act[1, f, r, :, 0:64] = v[:, 128:192]
    for f in range(3):
        for row in range(2):
            pieces = []
            for u in range(2):
                for w in range(2):
                    columns = pl.ds(w, 48, stride=2)
                    r = 2 * row + u
                    pieces += [act[0, f, r, columns, :], act[1, f, r, columns, :][:, :64]]
            pat[row, pl.ds(48 * f, 48)] = jnp.concatenate(pieces, axis=1).astype(BF16)

    def pat_copy(src, dst, sem, to):
        return remote(pat.at[src], pat.at[dst], pat_send.at[sem], pat_recv.at[dst], (tm, to))

    pat_copies = [
        pat_copy(0, 2, 0, h_up),
        pat_copy(1, 3, 1, h_down),
        pat_copy(1, 4, 2, h_up),
        pat_copy(0, 5, 3, h_down),
    ]
    pat_onward = [pat_copy(2, 6, 4, h_up), pat_copy(3, 7, 5, h_down)]
    order = [(0, 0), (0, 1), (3, 0), (1, 1), (3, 1), (1, 0), (2, 0), (2, 1)]
    for cp in pat_copies:
        cp.start()
    loads[2].wait()

    @pl.when(at_end)
    def _():
        wo_copy.wait_recv()
        wo_share.start()
        remote(wo.at[wo_rest], wo.at[wo_rest], wo_sem.at[2], wo_sem.at[3], dev(x, zl, 1 - c, y, zh)).wait_recv()

    def pat_wait(slot):
        remote(pat.at[slot], pat.at[slot], pat_send.at[0], pat_recv.at[slot], (tm, h_up)).wait_recv()

    own_part = pl.ds(pl.multiple_of(c * (HD // 2), HD // 2), HD // 2)
    ow_z = [
        remote(ow.at[h, own_part], ow.at[h, own_part], ow_send.at[6 + i], ow_recv.at[h], to)
        for i, to in enumerate((ow_near, ow_far))
    ]
    loads[7].wait()

    shift_row = mod[0:1, :]
    scale_row = 1.0 + mod[1:2, :]
    q_scale = HD ** (-0.5) * math.log2(math.e)

    def project(group):
        patches = pat[2 * group : 2 * group + 2].reshape(PIECE, 4 * CC)
        tokens = (jnp.dot(patches, pw[...], preferred_element_type=F32) + patch_b[...]).astype(BF16)
        if group == 0:

            @pl.when(zh == 0)
            def _():
                tok[...] = tokens[:ROW]

            @pl.when(zh == 1)
            def _():
                tok[...] = tokens[ROW:]

        wide = tokens.astype(F32)
        centered = wide - jnp.mean(wide, axis=-1, keepdims=True)
        variance = jnp.mean(centered * centered, axis=-1, keepdims=True)
        normed = (centered * lax.rsqrt(variance + 1e-06) * scale_row + shift_row).astype(BF16)
        qkv = jnp.dot(normed, wq[...], preferred_element_type=F32)
        rows = pl.ds(group * PIECE, PIECE)
        q_ref[rows, :] = (qkv[:, 0:HD] * q_scale).astype(BF16)
        kv[0, 0, rows, :] = qkv[:, HD : 2 * HD].astype(BF16)
        kv[0, 1, rows, :] = qkv[:, 2 * HD :].astype(BF16)

        @pl.when(at_end)
        def _():
            other = jnp.dot(normed, wo[...], preferred_element_type=F32).astype(BF16)
            kv_far[0, rows, :] = other[:, :HD]
            kv_far[1, rows, :] = other[:, HD:]

    def half_rows(g):
        return pl.ds(pl.multiple_of(g * HALF, HALF), HALF)

    def half_of(slot, g):
        return kv.at[slot, :, half_rows(g), :]

    def piece_of(slot, p):
        return kv.at[slot, :, pl.ds(pl.multiple_of(p * PIECE, PIECE), PIECE), :]

    z_next = dev(x, (zl + 1) % 4, c, y, zh)
    z_prev = dev(x, (zl + 3) % 4, c, y, zh)
    x_next = dev((x + 1) % 4, zl, c, y, zh)
    mate = dev(x, zl, 1 - c, y, zh)

    win_copies = []
    end_to = dev((x + zl // 3) % 4, 3 * (1 - zl // 3), c, y, 1 - zh)
    end_slot = 3 - 2 * (zl // 3)

    def send_own(p):
        up = remote(piece_of(0, p), piece_of(1, p), win_send.at[p], win_recv.at[1, p], z_next)
        across = remote(piece_of(0, p), piece_of(4, p), win_send.at[4 + p], win_recv.at[4, p], x_next)
        far = remote(
            kv_far.at[:, pl.ds(p * PIECE, PIECE)], piece_of(end_slot, p), far_send.at[p], win_recv.at[end_slot, p], end_to
        )
        across.start()

        @pl.when(zl < 3)
        def _():
            up.start()

        @pl.when(at_end)
        def _():
            far.start()

        win_copies.append((up, across, far))

    def passing_on(d, p):
        up = remote(piece_of(d, p), piece_of((d + 1) % 5, p), fwd_send.at[d - 1, p], win_recv.at[(d + 1) % 5, p], z_next)
        down = remote(piece_of(d, p), piece_of(d - 1, p), fwd_send.at[d - 1, p], win_recv.at[d - 1, p], z_prev)
        middle = jnp.logical_and(zl > 0, zl < 3)
        goes_up = jnp.logical_and(d == 1, middle)
        goes_down = jnp.logical_or(jnp.logical_and(d == 4, zl > 0), jnp.logical_and(d == 3, middle))
        return up, down, goes_up, goes_down

    def pass_on(d, p):
        remote(piece_of(0, p), piece_of(d, p), fwd_send.at[0, 0], win_recv.at[d, p], mate).wait_recv()
        up, down, goes_up, goes_down = passing_on(d, p)

        @pl.when(goes_up)
        def _():
            up.start()

        @pl.when(goes_down)
        def _():
            down.start()

    def share_copy(d, g):
        src = c * d + (1 - c) * (d % 4)
        dst = 4 + c * d + (1 - c) * (d % 4 + 1)
        return remote(half_of(src, g), half_of(dst, g), mate_send.at[d - 1, g], win_recv.at[dst, g], mate)

    project(0)
    send_own(0)

    @pl.when(at_end)
    def _():
        for cp in ow_z:
            cp.start()

    pat_wait(2)
    pat_onward[0].start()
    pat_wait(3)
    pat_onward[1].start()
    project(1)
    send_own(1)
    pat_wait(4)
    pat_wait(5)
    project(2)
    send_own(2)
    for d in (1, 4):
        pass_on(d, 0)
    pat_wait(6)
    pat_wait(7)
    project(3)
    send_own(3)
    for d in (1, 4):
        pass_on(d, 1)
        share_copy(d, 0).start()
    pass_on(3, 0)

    def ow_sends(row, first):
        part = ow.at[row, own_part]
        return [
            remote(part, part, ow_send.at[first + k], ow_recv.at[row], (tm, ((y + k + 1) % 4) * 2 + zh)) for k in (0, 2, 1)
        ]

    def ow_wait(row):
        part = ow.at[row, own_part]
        remote(part, part, ow_send.at[0], ow_recv.at[row], (tm, h_up)).wait_recv()

    def ow_share(row):
        part = ow.at[row, own_part]
        return remote(part, part, share_send.at[row], share_recv.at[row], mate)

    h_other = y * 2 + 1 - zh
    ow_copies = ow_sends(h, 0) + ow_sends(h_other, 3)
    for cp in ow_copies[:3]:
        cp.start()
    others = [h_other] + [((y + k) % 4) * 2 + half for k in range(1, 4) for half in range(2)]

    q_cols[...] = q_ref[...].astype(F32).T.astype(BF16)
    acc[...] = jnp.zeros_like(acc)
    col_sum[...] = jnp.zeros_like(col_sum)
    col_max[...] = jnp.full_like(col_max, NEG)

    def attend(slot, g, back):
        penalty = jnp.where(back <= lookback[0], 0.0, 1e30)
        values = kv[slot, 1, half_rows(g), :].T
        scores = jnp.dot(kv[slot, 0, half_rows(g), :], q_cols[...], preferred_element_type=F32)
        old = col_max[...]
        new = jnp.maximum(old, jnp.max(scores, axis=0, keepdims=True) - penalty)
        probs = jnp.exp2(scores - (new + penalty))
        shrink = jnp.exp2(old - new)
        col_max[...] = new
        col_sum[...] = col_sum[...] * shrink + jnp.sum(probs, axis=0, keepdims=True)
        acc[...] = acc[...] * shrink + jnp.dot(values, probs.astype(BF16), preferred_element_type=F32)

    arrivals = [(1, 0), (4, 0), (3, 0), (1, 1), (4, 1), (3, 1), (2, 0), (2, 1)]
    code = sum(((d - 1) * 2 + g) * 8**i for i, (d, g) in enumerate(arrivals))
    steps_of = {
        0: ([(1, 2), (4, 2)], []),
        1: ([(3, 1)], [(3, 0)]),
        2: ([(1, 3), (4, 3)], [(1, 1), (4, 1)]),
        3: ([(3, 2)], []),
        5: ([(3, 3)], [(3, 1)]),
        8: ([(2, 0), (2, 1)], [(2, 0)]),
        12: ([(2, 2), (2, 3)], [(2, 1)]),
    }

    def event(n, code):
        @pl.when(n == 3)
        def _():
            ow_wait(h_other)
            for cp in ow_copies[3:]:
                cp.start()

        @pl.when(n == 7)
        def _():
            for row in others[1:]:
                ow_wait(row)
            for row in others:
                ow_share(row).start()

        first = (8 - n) // 8
        digit = code % 8
        d = (1 - first) * (digit // 2 + 1)
        g = (1 - first) * (digit % 2)
        got = 4 + (1 - c) * d + c * (d % 4 + 1)

        def one(k, _):
            for at, (passed, shared) in steps_of.items():

                @pl.when(2 * n + k == at)
                def _(passed=passed, shared=shared):
                    for d, p in passed:
                        pass_on(d, p)
                    for d, g in shared:
                        share_copy(d, g).start()

            @pl.when(jnp.logical_and(n > 0, k == 1))
            def _():
                remote(half_of(0, g), half_of(got, g), mate_send.at[0, 0], win_recv.at[got, g], mate).wait_recv()

            slot = (1 - k) * d + k * (1 - first) * got
            back = jnp.where(slot <= 4, 2 * slot, 2 * slot - 9)
            attend(slot, g + k * first, back)
            return 0

        lax.fori_loop(0, 2, one, 0)
        return first * code + (1 - first) * (code // 8)

    lax.fori_loop(0, 9, event, code)

    def mix_copy(s):
        to = ((y + order[s][0]) % 4) * 2 + order[s][1]
        return to, remote(obuf.at[s], mix.at[h], mix_send.at[s], mix_recv.at[h], (tm, to))

    all_out = (acc[...] / col_sum[...]).T.astype(BF16)
    for s in range(8):
        heads_out = all_out[s * ROW : (s + 1) * ROW]
        obuf[s] = heads_out
        to, cp = mix_copy(s)

        @pl.when(to == h)
        def _(heads_out=heads_out):
            mix[h] = heads_out

        @pl.when(to != h)
        def _(cp=cp):
            cp.start()

    for row in others:
        part = ow.at[row, pl.ds(pl.multiple_of((1 - c) * (HD // 2), HD // 2), HD // 2)]
        remote(part, part, share_send.at[row], share_recv.at[row], mate).wait_recv()
    for k in range(1, 8):
        r = (h + k) % 8
        remote(obuf.at[0], mix.at[r], mix_send.at[0], mix_recv.at[r], (tm, h_up)).wait_recv()
    heads = jnp.concatenate([mix[i] for i in range(8)], axis=1)
    attended = jnp.dot(heads, ow[...].reshape(8 * HD, D), preferred_element_type=F32)
    refined = (tok[...].astype(F32) + mod[2:3, :] * attended).astype(BF16)
    out[...] = refined.reshape(3, 1, 48, D)

    for cp in halo + halo_more + list(z_copies.values()) + pat_copies + pat_onward + ow_copies:
        cp.wait_send()
    for row in others:
        ow_share(row).wait_send()

    @pl.when(at_end)
    def _():
        for cp in ow_z + [wo_copy, wo_share] + [far for _, _, far in win_copies]:
            cp.wait_send()

    for up, across, _ in win_copies:
        across.wait_send()

        @pl.when(zl < 3)
        def _(up=up):
            up.wait_send()

    def drain(i, _):
        d = i // 4 + 1
        up, down, goes_up, goes_down = passing_on(d, i % 4)

        @pl.when(goes_up)
        def _():
            up.wait_send()

        @pl.when(goes_down)
        def _():
            down.wait_send()

        return 0

    lax.fori_loop(0, 16, drain, 0)
    for d in range(1, 5):
        for g in range(2):
            share_copy(d, g).wait_send()

    for s in range(8):
        to, cp = mix_copy(s)

        @pl.when(to != h)
        def _(cp=cp):
            cp.wait_send()


def on_device(
    feats, conv_weight, conv_bias, patch_weight, patch_bias, time_weight, qkv_weight, out_weight, steps_index, lookback
):
    vmem = pl.BlockSpec(memory_space=pltpu.VMEM)
    smem = pl.BlockSpec(memory_space=pltpu.SMEM)
    hbm = pl.BlockSpec(memory_space=pl.ANY)
    dma = pltpu.SemaphoreType.DMA
    return pl.pallas_call(
        kernel,
        out_shape=jax.ShapeDtypeStruct((3, 1, 48, D), BF16),
        in_specs=[hbm, hbm, vmem, hbm, vmem, hbm, hbm, hbm, smem, smem],
        out_specs=vmem,
        scratch_shapes=[
            pltpu.VMEM((3, 96, 2 * CC), BF16),
            pltpu.VMEM((3, 96, 2 * CC), BF16),
            pltpu.VMEM((5, 6, 96, CC), BF16),
            pltpu.VMEM((3, 3, 3, CC, CC), BF16),
            pltpu.VMEM((4 * CC, D), BF16),
            pltpu.VMEM((FREQ, 3 * D), F32),
            pltpu.VMEM((D, 3 * HD), BF16),
            pltpu.VMEM((D, 2 * HD), BF16),
            pltpu.VMEM((8, HD, D), BF16),
            pltpu.VMEM((3, 3, 4, 112, CC), F32),
            pltpu.VMEM((2, 3, 4, 96, 128), F32),
            pltpu.VMEM((8, ROW, 4 * CC), BF16),
            pltpu.VMEM((ROW, D), BF16),
            pltpu.VMEM((3, D), F32),
            pltpu.VMEM((NTOK, HD), BF16),
            pltpu.VMEM((HD, NTOK), BF16),
            pltpu.VMEM((9, 2, NTOK, HD), BF16),
            pltpu.VMEM((2, NTOK, HD), BF16),
            pltpu.VMEM((HD, NTOK), F32),
            pltpu.VMEM((1, NTOK), F32),
            pltpu.VMEM((1, NTOK), F32),
            pltpu.VMEM((8, ROW, HD), BF16),
            pltpu.VMEM((8, ROW, HD), BF16),
            dma((8,)),
            dma((3,)),
            dma((3,)),
            dma((6,)),
            dma((6,)),
            dma((6,)),
            dma((8,)),
            dma((8,)),
            dma((9, 4)),
            dma((4, 4)),
            dma((4, 2)),
            dma((4,)),
            dma((4,)),
            dma((8,)),
            dma((8,)),
            dma((8,)),
            dma((8,)),
            dma((8,)),
            dma((8,)),
        ],
        compiler_params=pltpu.CompilerParams(
            collective_id=0, has_side_effects=True, vmem_limit_bytes=56 * 1024 * 1024
        ),
        name="block",
    )(
        feats, conv_weight, conv_bias, patch_weight, patch_bias, time_weight,
        qkv_weight, out_weight, steps_index, lookback,
    )


def solution(mesh):
    in_specs = (
        P("tm", "height", None, None),
        P(),
        P(),
        P(),
        P(),
        P(),
        P(None, None, "height"),
        P("height", None),
        P("tm"),
        P("tm"),
    )
    out_specs = P("tm", "height", None, None)
    return jax.shard_map(
        on_device, mesh=mesh, in_specs=in_specs, out_specs=out_specs, check_vma=False
    )
```
